256 devices in a mesh: bead: 8 (over x, core), space: 32 (over z, y).
Axes of the slice: x: 4, y: 4, z: 8, core: 2. Of those that a mesh axis runs over, the one named last changes fastest.
Arguments:
- charges: float32 [32, 512, 128, 128], P('bead', 'space'), parts along dimension 0, may hold values from -6 to 6
- kernel_taps: float32 [4, 4, 3, 15], replicated, may hold values from -1.5 to 1.5
Outputs:
- potential: float32 [32, 512, 128, 128], P('bead', 'space'), parts along dimension 0
The draws below stay inside these ranges and needn't reach their ends.
There are 8 independent parts, one for each index of `bead`. The reference program is written for one: setup_inputs(seed, part) draws one part's arguments, and reference() takes and returns one part's arrays. A program takes and returns all parts, laid end to end along the dimension named above; an argument that names none is the same for every part. Nothing has to cross between parts.
All inputs are finite; a program needn't handle non-finite values.
Results may differ from the reference program's by a relative error of at most 0.0001.
Values sent between devices are 32-bit elements; how exact they have to be, the bound alone decides.
No kernel may reach another device: no remote copies, remote signals or barrier semaphores. Data moves between devices by JAX's collectives and lax.ppermute only.
A program may use at most 128 MiB of HBM per device.

```python
import jax
import jax.numpy as jnp
from jax import lax

BEADS = 4
NXY = 128
LEVELS = 4
TERMS = 4
REACH = 7
NZ = 512


def level_of(key, dims, split, least, top_value):
    def one(dim, shards_of):
        heights = jax.random.uniform(jax.random.fold_in(jax.random.fold_in(key, 6), dim), (shards_of,), jnp.float32, least / len(split), top_value / len(split))
        return jnp.repeat(jnp.exp(heights), dims[dim] // shards_of).reshape((-1,) + (1,) * (len(dims) - dim - 1))

    loudness = one(*split[0])
    for cut in split[1:]:
        loudness = loudness * one(*cut)
    return loudness


def normal_values(stream_key, dims, scale, limit, pieces=(), kind=jnp.bfloat16):
    entries = jax.random.normal(stream_key, dims, jnp.float32) * scale
    if len(pieces) > 0:
        entries = level_of(stream_key, dims, pieces, -0.22, 0.18) * entries
    return jnp.clip(entries, min=-limit, max=limit).astype(kind)


def setup_inputs(seed: int = 0, part: int = 0) -> dict:
    arg_keys = jax.random.split(jax.random.key(seed), 3)
    own_keys = jax.random.split(jax.random.fold_in(arg_keys[2], part), 3)
    return {
        "charges": normal_values(own_keys[0], (BEADS, NZ, NXY, NXY), 1.0, 6.0, ((1, 32),), jnp.float32),
        "kernel_taps": normal_values(arg_keys[1], (LEVELS, TERMS, 3, 2 * REACH + 1), (2 * REACH + 1) ** -0.5, 1.5, (), jnp.float32),
    }


exact_precision = lax.Precision.HIGHEST
cubic_taps = ((0, 1.0), (1, 0.5625), (-1, 0.5625), (3, -0.0625), (-3, -0.0625))


def coarsen_axis(grid_field, axis_index):
    summed = jnp.zeros_like(grid_field)
    for offset, weight in cubic_taps:
        summed = summed + (0.5 * weight) * jnp.roll(grid_field, -offset, axis=axis_index)
    return lax.slice_in_dim(summed, 0, summed.shape[axis_index], 2, axis_index)


def refine_axis(coarse_field, axis_index):
    config = [(0, 0, 0)] * coarse_field.ndim
    config[axis_index] = (0, 1, 1)
    spread = lax.pad(coarse_field, jnp.array(0.0, coarse_field.dtype), config)
    summed = jnp.zeros_like(spread)
    for offset, weight in cubic_taps:
        summed = summed + weight * jnp.roll(spread, offset, axis=axis_index)
    return summed


def circulant(kernel_row, side_len):
    identity = jnp.eye(side_len, dtype=jnp.float32)
    summed = jnp.zeros((side_len, side_len), jnp.float32)
    for tap_index in range(2 * REACH + 1):
        summed = summed + kernel_row[tap_index] * jnp.roll(identity, tap_index - REACH, axis=1)
    return summed


def convolve_level(grid_field, level_taps):
    summed = jnp.zeros_like(grid_field)
    side_len = grid_field.shape[2]
    for term_index in range(level_taps.shape[0]):
        term_field = jnp.zeros_like(grid_field)
        for tap_index in range(2 * REACH + 1):
            term_field = term_field + level_taps[term_index, 0, tap_index] * jnp.roll(grid_field, REACH - tap_index, axis=1)
        along_y = circulant(level_taps[term_index, 1], side_len)
        along_x = circulant(level_taps[term_index, 2], side_len)
        term_field = jnp.einsum("yv,bzvx->bzyx", along_y, term_field, precision=exact_precision)
        term_field = jnp.einsum("xv,bzyv->bzyx", along_x, term_field, precision=exact_precision)
        summed = summed + term_field
    return summed


def reference(charges, kernel_taps):
    level_charges = [charges]
    for level_index in range(1, LEVELS):
        coarse = level_charges[-1]
        for axis_index in (1, 2, 3):
            coarse = coarsen_axis(coarse, axis_index)
        level_charges.append(coarse)
    potential_field = convolve_level(level_charges[LEVELS - 1], kernel_taps[LEVELS - 1])
    for level_index in range(LEVELS - 2, -1, -1):
        refined = potential_field
        for axis_index in (1, 2, 3):
            refined = refine_axis(refined, axis_index)
        potential_field = convolve_level(level_charges[level_index], kernel_taps[level_index]) + refined
    return potential_field
```

```python
import functools

import jax
import jax.numpy as jnp
import ml_dtypes
import numpy as np
from jax import lax
from jax.experimental import pallas as pl
from jax.experimental.pallas import tpu as pltpu
from jax.sharding import PartitionSpec as P

REACH = 7
TAPS = 15
SIDE = 128
SLAB = 16
COUNT = 32
CHUNKS = ((0, 3), (3, 2), (5, 2))
F32 = jnp.float32
BF16 = jnp.bfloat16
CUBIC = {0: 1.0, 1: 0.5625, -1: 0.5625, 3: -0.0625, -3: -0.0625}


def symbol(side):
    theta = 2.0 * np.pi * np.arange(side) / side
    return 1.0 + 1.125 * np.cos(theta) - 0.125 * np.cos(3.0 * theta)


def split_const(matrix):
    high = matrix.astype(ml_dtypes.bfloat16)
    low = (matrix - high.astype(np.float64)).astype(ml_dtypes.bfloat16)
    return high, low


def dft_parts():
    angle = 2.0 * np.pi * (np.outer(np.arange(SIDE), np.arange(SIDE)) % SIDE) / SIDE
    c, s = np.cos(angle), np.sin(angle)
    fwd_x = np.block([[c, -s], [s, c]])
    fwd_y = np.block([[c, s], [-s, c]])
    inv_y = np.block([[c, -s], [s, c]]) / SIDE
    inv_x = np.block([[c, s], [-s, c]]) / SIDE
    return [part for m in (fwd_x, fwd_y, inv_y, inv_x) for part in split_const(m)]


def fold_weights():
    full = np.outer(symbol(128), symbol(128)) / 16.0
    half = np.outer(symbol(64), symbol(64)) / 16.0
    quarter = np.outer(symbol(32), symbol(32)) / 16.0
    half = np.tile(half, (1, 2))
    quarter = np.concatenate([quarter, quarter * 0, quarter, quarter * 0], axis=1)
    return full.astype(np.float32), half.astype(np.float32), quarter.astype(np.float32)


def spread_weights():
    full = np.outer(symbol(128), symbol(128))
    half = np.tile(np.outer(symbol(64), symbol(64)), (1, 2))
    return full.astype(np.float32), half.astype(np.float32)


def split(value):
    high = value.astype(BF16)
    return high, (value - high.astype(F32)).astype(BF16)


def dot(a, b):
    return jnp.dot(a, b, preferred_element_type=F32)


def right_mul(value, high, low):
    vh, vl = split(value)
    return dot(vh, high) + dot(vl, high) + dot(vh, low)


def left_mul(high, low, value):
    vh, vl = split(value)
    return dot(high, vh) + dot(high, vl) + dot(low, vh)


def params(megabytes=40):
    return pltpu.CompilerParams(vmem_limit_bytes=megabytes * 1024 * 1024)


def whole(shape):
    return pl.BlockSpec(shape, lambda *_: (0,) * len(shape))


def forward_kernel(v_low, v_high, xh, xl, yh, yl, out_low, out_high):
    for v, out in ((v_low, out_low), (v_high, out_high)):
        rows = jnp.concatenate(
            [jnp.concatenate([v[0, 0], v[1, 0]], 1), jnp.concatenate([v[2, 0], v[3, 0]], 1)], 0
        )
        a = right_mul(rows, xh[...], xl[...])
        b = jnp.concatenate(
            [
                jnp.concatenate([a[:SIDE, :SIDE], a[:SIDE, SIDE:]], 0),
                jnp.concatenate([a[SIDE:, :SIDE], a[SIDE:, SIDE:]], 0),
            ],
            1,
        )
        c = left_mul(yh[...], yl[...], b)
        out[0, 0, 0] = c[:SIDE, :SIDE]
        out[0, 0, 1] = c[SIDE:, :SIDE]
        out[0, 1, 0] = c[:SIDE, SIDE:]
        out[0, 1, 1] = c[SIDE:, SIDE:]


def forward(charges, first, layers, mats):
    top = SLAB - first - layers
    shape = jax.ShapeDtypeStruct((layers, 2, 2, SIDE, SIDE), F32)
    block = pl.BlockSpec((1, 2, 2, SIDE, SIDE), lambda i: (i, 0, 0, 0, 0))
    return pl.pallas_call(
        forward_kernel,
        grid=(layers,),
        in_specs=[
            pl.BlockSpec((4, 1, SIDE, SIDE), lambda i: (0, first + i, 0, 0)),
            pl.BlockSpec((4, 1, SIDE, SIDE), lambda i: (0, top + i, 0, 0)),
        ]
        + [whole((256, 256))] * 4,
        out_specs=[block, block],
        out_shape=[shape, shape],
        compiler_params=params(),
        name="forward",
        cost_estimate=pl.CostEstimate(
            flops=layers * 4 * 3 * 2 * 2 * 128 * 256 * 256, bytes_accessed=layers * 4 * 4 * 65536, transcendentals=0
        ),
    )(charges, charges, *mats[:4])


def piece_of(z):
    for k, (first, layers) in enumerate(CHUNKS + ((7, 1),)):
        if first <= z < first + layers:
            return 2 * k, z - first
        top = SLAB - first - layers
        if top <= z < top + layers:
            return 2 * k + 1, z - top
    return None


def piece_specs(rows):
    specs = []
    for _, layers in CHUNKS + ((7, 1),):
        specs += [pl.BlockSpec((layers, 2, 2, rows, SIDE), lambda r: (0, 0, 0, r, 0))] * 2
    return specs


def fold_lanes(value, lanes):
    return value + pltpu.roll(value, SIDE - lanes, 1)


def restrict_layers(layers, first, low, high):
    out = []
    for cell in range(low, high):
        total = None
        for d, weight in CUBIC.items():
            z = 2 * cell + d - first
            if 0 <= z < len(layers):
                term = (0.5 * weight) * layers[z]
                total = term if total is None else total + term
        out.append(total)
    return out


def partial_kernel(*refs):
    pieces = refs[:8]
    full, half, quarter = refs[8:11]
    up_ref, down_ref, own_ref, pay_ref = refs[11:15]
    fine_ref, mid_ref = refs[15:17]
    lane = lax.broadcasted_iota(jnp.int32, (64, SIDE), 1)
    for z in range(SLAB):
        k, i = piece_of(z)
        for part in range(2):
            sides = []
            for pair in range(2):
                g = full[...] * pieces[k][i, pair, part]
                g = g[:64] + g[64:]
                sides.append(fold_lanes(g, 64))
            fine_ref[z, 64 * part : 64 * part + 64] = jnp.where(lane < 64, sides[0], sides[1])

    cells = restrict_layers([fine_ref.at[z] for z in range(SLAB)] and [fine_ref[z] for z in range(SLAB)], 0, -1, 10)
    for c, value in zip(range(-1, 10), cells):
        mid_ref[c + 1] = value
        if 0 <= c <= 8:
            own_ref[c] = value
        if c in (8, 9):
            up_ref[c - 8] = value
        if c in (-1, 0):
            down_ref[c + 1] = value

    small = []
    for c in range(11):
        parts = []
        for part in range(2):
            g = half[...] * mid_ref[c, 64 * part : 64 * part + 64]
            parts.append(fold_lanes(g[:32] + g[32:], 32))
        small.append(jnp.concatenate(parts, 0))
    level2 = restrict_layers(small, -1, -2, 7)
    lane = lax.broadcasted_iota(jnp.int32, (32, SIDE), 1)
    for c, value in enumerate(level2):
        packed = jnp.where((lane // 32) % 2 == 0, value[:32], pltpu.roll(value[32:], 32, 1))
        pay_ref[:, c, :] = packed

    tiny = []
    for value in level2:
        parts = []
        for part in range(2):
            g = quarter[...] * value[32 * part : 32 * part + 32]
            parts.append(fold_lanes(g[:16] + g[16:], 16))
        tiny.append(jnp.concatenate(parts, 0))
    level3 = restrict_layers(tiny, -2, -2, 5)
    lane = lax.broadcasted_iota(jnp.int32, (16, SIDE), 1)
    for c, value in enumerate(level3):
        packed = jnp.where((lane // 16) % 2 == 0, value[:16], pltpu.roll(value[16:], 16, 1))
        pay_ref[:, 9 + c, :] = jnp.concatenate([packed, packed], 0)


def partial_sums(pieces):
    outs = [(2, SIDE, SIDE), (2, SIDE, SIDE), (9, SIDE, SIDE), (COUNT, 16, SIDE)]
    return pl.pallas_call(
        partial_kernel,
        out_shape=[jax.ShapeDtypeStruct(s, F32) for s in outs],
        scratch_shapes=[pltpu.VMEM((SLAB, SIDE, SIDE), F32), pltpu.VMEM((11, SIDE, SIDE), F32)],
        compiler_params=params(),
        name="partial",
        cost_estimate=pl.CostEstimate(flops=4000000, bytes_accessed=6000000, transcendentals=0),
    )(*pieces, *[jnp.asarray(w) for w in fold_weights()])


def gather_matrix():
    out = np.zeros((144 + 80, COUNT * 16))
    for src in range(COUNT):
        for c in range(9):
            z = (4 * src + c - 2) % 128
            for r in range(142):
                if (r - 7) % 128 == z:
                    out[r, src * 16 + c] = 1.0
        for c in range(7):
            z = (2 * src + c - 2) % 64
            for r in range(78):
                if (r - 7) % 64 == z:
                    out[144 + r, src * 16 + 9 + c] = 1.0
    return out.astype(ml_dtypes.bfloat16)


def scatter_matrix():
    prolong = np.zeros((128, 64))
    for j in range(64):
        for d, weight in CUBIC.items():
            prolong[(2 * j + d) % 128, j] += weight
    table = np.concatenate([np.eye(128), prolong], axis=1)
    out = np.zeros((COUNT * 16, 192))
    for dst in range(COUNT):
        for c in range(9):
            out[dst * 16 + c] = table[(4 * dst + c - 2) % 128]
    return out.astype(ml_dtypes.bfloat16)


def swap_lanes(value, lanes):
    lane = lax.broadcasted_iota(jnp.int32, value.shape, 1)
    return jnp.where((lane // lanes) % 2 == 0, pltpu.roll(value, SIDE - lanes, 1), pltpu.roll(value, lanes, 1))


def along_kernel(x_ref, gather, scatter, a2, b2, a3, b3, spread, out_ref, c_ref, s_ref):
    xh, xl = split(x_ref[...])
    c_ref[...] = dot(gather[...], xh) + dot(gather[...], xl)
    s_ref[:144] = swap_lanes(c_ref[:144], 32)
    s_ref[144:] = swap_lanes(c_ref[144:], 16)
    p2 = jnp.zeros((128, SIDE), F32)
    p3 = jnp.zeros((64, SIDE), F32)
    for t in range(TAPS):
        p2 = p2 + a2[t : t + 1] * c_ref[t : t + 128] + b2[t : t + 1] * s_ref[t : t + 128]
        p3 = p3 + a3[t : t + 1] * c_ref[144 + t : 208 + t] + b3[t : t + 1] * s_ref[144 + t : 208 + t]
    block = (lax.broadcasted_iota(jnp.int32, p3.shape, 1) // 16) % 4
    wide = jnp.where(block == 0, p3, jnp.where(block == 3, pltpu.roll(p3, 32, 1), pltpu.roll(p3, 16, 1)))
    wide = spread[...] * wide
    both = jnp.concatenate([p2, wide], 0)
    bh, bl = split(both)
    out_ref[...] = dot(scatter[...], bh) + dot(scatter[...], bl)


def along_z(received, coefs):
    return pl.pallas_call(
        along_kernel,
        out_shape=jax.ShapeDtypeStruct((COUNT * 16, SIDE), F32),
        scratch_shapes=[pltpu.VMEM((224, SIDE), F32), pltpu.VMEM((224, SIDE), F32)],
        compiler_params=params(),
        name="along",
        cost_estimate=pl.CostEstimate(flops=30000000, bytes_accessed=2000000, transcendentals=0),
    )(received, jnp.asarray(gather_matrix()), jnp.asarray(scatter_matrix()), *coefs)


def level_kernel(below, own, above, w_ref, y_ref, spread, out_ref, p_ref):
    def cell_ref(c):
        if c < 0:
            return below, c + 8
        if c <= 8:
            return own, c
        return above, c - 9

    def block(r, carry):
        rows = pl.ds(pl.multiple_of(8 * r, 8), 8)
        lower = pl.ds(pl.multiple_of(64 + 8 * r, 8), 8)
        for c in range(-1, 10):
            re = im = None
            for t in range(TAPS):
                ref, i = cell_ref(c + t - REACH)
                wr, wi = w_ref[t, rows], w_ref[t, lower]
                vr, vi = ref[i, rows], ref[i, lower]
                nr = wr * vr - wi * vi
                ni = wr * vi + wi * vr
                re = nr if re is None else re + nr
                im = ni if im is None else im + ni
            p_ref[c + 1, rows] = re
            p_ref[c + 1, lower] = im
        return carry

    lax.fori_loop(0, 8, block, 0)

    lane = lax.broadcasted_iota(jnp.int32, (32, SIDE), 1)
    low = (lane // 32) % 2 == 0
    wides = []
    for c in range(9):
        y = y_ref[:, c, :]
        re = jnp.where(low, y, pltpu.roll(y, 32, 1))
        im = jnp.where(low, pltpu.roll(y, SIDE - 32, 1), y)
        wides.append((re, im))
    for c in range(-1, 10):
        for part in range(2):
            total = None
            for d, weight in CUBIC.items():
                if (c - d) % 2 == 0 and -2 <= (c - d) // 2 <= 6:
                    term = weight * wides[(c - d) // 2 + 2][part]
                    total = term if total is None else total + term
            for tile in range(2):
                rows = slice(64 * part + 32 * tile, 64 * part + 32 * tile + 32)
                p_ref[c + 1, rows] += spread[32 * tile : 32 * tile + 32] * total
    for z in range(SLAB):
        total = None
        for d, weight in CUBIC.items():
            if (z - d) % 2 == 0:
                term = weight * p_ref[(z - d) // 2 + 1]
                total = term if total is None else total + term
        out_ref[z] = total


def level_one(below, own, above, w1, y):
    return pl.pallas_call(
        level_kernel,
        out_shape=jax.ShapeDtypeStruct((SLAB, SIDE, SIDE), F32),
        scratch_shapes=[pltpu.VMEM((11, SIDE, SIDE), F32)],
        compiler_params=params(),
        name="level",
        cost_estimate=pl.CostEstimate(flops=40000000, bytes_accessed=5000000, transcendentals=0),
    )(below, own, above, w1, y, jnp.asarray(spread_weights()[1]))


CONV_ROWS = 16


def local_kernel(*refs):
    pieces, w_ref, out_ref = refs[:8], refs[8], refs[9]

    def block(r, carry):
        rows = pl.ds(pl.multiple_of(8 * r, 8), 8)
        for z in range(SLAB):
            acc = [None] * 4
            for t in range(TAPS):
                src = z + t - REACH
                if not 0 <= src < SLAB:
                    continue
                k, i = piece_of(src)
                wr, wi = w_ref[t, 0, rows], w_ref[t, 1, rows]
                for pair in range(2):
                    vr, vi = pieces[k][i, pair, 0, rows], pieces[k][i, pair, 1, rows]
                    nr = wr * vr - wi * vi
                    ni = wr * vi + wi * vr
                    acc[2 * pair] = nr if acc[2 * pair] is None else acc[2 * pair] + nr
                    acc[2 * pair + 1] = ni if acc[2 * pair + 1] is None else acc[2 * pair + 1] + ni
            for pair in range(2):
                out_ref[z, pair, 0, rows] = acc[2 * pair]
                out_ref[z, pair, 1, rows] = acc[2 * pair + 1]
        return carry

    lax.fori_loop(0, CONV_ROWS // 8, block, 0)


def local_sums(pieces, w0):
    return pl.pallas_call(
        local_kernel,
        grid=(SIDE // CONV_ROWS,),
        in_specs=piece_specs(CONV_ROWS) + [pl.BlockSpec((TAPS, 2, CONV_ROWS, SIDE), lambda r: (0, 0, r, 0))],
        out_specs=pl.BlockSpec((SLAB, 2, 2, CONV_ROWS, SIDE), lambda r: (0, 0, 0, r, 0)),
        out_shape=jax.ShapeDtypeStruct((SLAB, 2, 2, SIDE, SIDE), F32),
        compiler_params=params(),
        name="local",
        cost_estimate=pl.CostEstimate(flops=120000000, bytes_accessed=10000000, transcendentals=0),
    )(*pieces, w0)


def finish_kernel(layer, first_steps, chunks, with_coarse, with_inverse, *refs):
    refs = list(refs)
    acc = refs.pop(0)
    halos = [(refs.pop(0), refs.pop(0)) for _ in chunks]
    w_ref = refs.pop(0)
    if with_coarse:
        coarse, spread = refs.pop(0), refs.pop(0)
    if with_inverse:
        yh, yl, xh, xl = (refs.pop(0) for _ in range(4))
        if first_steps is not None:
            refs.pop(0)
    out = refs.pop(0)
    total = refs.pop(0) if with_inverse else out
    z = layer(pl.program_id(0))
    total[...] = acc[...]

    def add(ref, i, tap):
        def block(r, carry):
            rows = pl.ds(pl.multiple_of(8 * r, 8), 8)
            wr, wi = w_ref[tap, 0, rows], w_ref[tap, 1, rows]
            for pair in range(2):
                vr, vi = ref[i, pair, 0, rows], ref[i, pair, 1, rows]
                total[0, pair, 0, rows] += wr * vr - wi * vi
                total[0, pair, 1, rows] += wr * vi + wi * vr
            return carry

        lax.fori_loop(0, SIDE // 8, block, 0, unroll=4)

    for (first, layers), (lower, upper) in zip(chunks, halos):
        for i in range(layers):
            from_below = -(first + layers) + i
            from_above = SLAB + first + i
            tap_below = from_below - z + REACH
            tap_above = from_above - z + REACH

            @pl.when(tap_below >= 0)
            def _():
                add(lower, i, tap_below)

            @pl.when(tap_above < TAPS)
            def _():
                add(upper, i, tap_above)

    if with_coarse:
        lane = lax.broadcasted_iota(jnp.int32, (64, SIDE), 1)
        for part in range(2):
            g = coarse[0, 64 * part : 64 * part + 64]
            h = pltpu.roll(g, 64, 1)
            for pair in range(2):
                tile = jnp.where((lane < 64) == (pair == 0), g, h)
                for row in (0, 64):
                    total[0, pair, part, row : row + 64] += spread[row : row + 64] * tile

    if with_inverse:
        b = jnp.concatenate(
            [jnp.concatenate([total[0, pair, 0], total[0, pair, 1]], 0) for pair in range(2)], 1
        )
        c = left_mul(yh[...], yl[...], b)
        rows = jnp.concatenate(
            [jnp.concatenate([c[:SIDE, SIDE * p : SIDE * p + SIDE], c[SIDE:, SIDE * p : SIDE * p + SIDE]], 1) for p in range(2)],
            0,
        )
        d = right_mul(rows, xh[...], xl[...])
        for pair in range(2):
            out[2 * pair, 0] = d[SIDE * pair : SIDE * pair + SIDE, :SIDE]
            out[2 * pair + 1, 0] = d[SIDE * pair : SIDE * pair + SIDE, SIDE:]


def finish(first, count, acc, acc_local, chunks, halos, w0, coarse, mats, result):
    contiguous = first + count == SLAB // 2
    steps = 2 * count

    def layer(i):
        if contiguous:
            return first + i
        return first + i + jnp.where(i >= count, SLAB - 2 * first - 2 * count, 0)

    operands = [acc]
    slot = (lambda i: (i, 0, 0, 0, 0)) if acc_local else (lambda i: (layer(i), 0, 0, 0, 0))
    specs = [pl.BlockSpec((1, 2, 2, SIDE, SIDE), slot)]
    for (_, layers), pair in zip(chunks, halos):
        operands += list(pair)
        specs += [whole((layers, 2, 2, SIDE, SIDE))] * 2
    operands.append(w0)
    specs.append(whole((TAPS, 2, SIDE, SIDE)))
    if coarse is not None:
        operands += [coarse, jnp.asarray(spread_weights()[0])]
        specs += [pl.BlockSpec((1, SIDE, SIDE), lambda i: (layer(i), 0, 0)), whole((SIDE, SIDE))]
    aliases = {}
    if mats is not None:
        operands += list(mats[4:])
        specs += [whole((256, 256))] * 4
        if result is not None:
            aliases = {len(operands): 0}
            operands.append(result)
            specs.append(pl.BlockSpec(memory_space=pl.ANY))
        out_spec = pl.BlockSpec((4, 1, SIDE, SIDE), lambda i: (0, layer(i), 0, 0))
        out_shape = jax.ShapeDtypeStruct((4, SLAB, SIDE, SIDE), F32)
        scratch = [pltpu.VMEM((1, 2, 2, SIDE, SIDE), F32)]
    else:
        out_spec = pl.BlockSpec((1, 2, 2, SIDE, SIDE), lambda i: (i, 0, 0, 0, 0))
        out_shape = jax.ShapeDtypeStruct((steps, 2, 2, SIDE, SIDE), F32)
        scratch = []
    return pl.pallas_call(
        functools.partial(
            finish_kernel, layer, None if result is None else 0, tuple(chunks), coarse is not None, mats is not None
        ),
        grid=(steps,),
        in_specs=specs,
        out_specs=out_spec,
        out_shape=out_shape,
        scratch_shapes=scratch,
        input_output_aliases=aliases,
        compiler_params=params(),
        name="finish",
        cost_estimate=pl.CostEstimate(flops=steps * 200000000, bytes_accessed=steps * 1000000, transcendentals=0),
    )(*operands)


def shifted(value, steps):
    pairs = [(source, (source + steps) % COUNT) for source in range(COUNT)]
    return lax.ppermute(value, "space", pairs)


def tap_waves(taps, side):
    angle = 2.0 * np.pi * np.outer(np.arange(TAPS) - REACH, np.arange(side)) / side
    cos = jnp.asarray(np.cos(angle), F32)
    sin = jnp.asarray(np.sin(angle), F32)
    exact = lax.Precision.HIGHEST
    return jnp.dot(taps, cos, precision=exact), jnp.dot(taps, sin, precision=exact)


def kernel_waves(level_taps, side):
    yr, yi = tap_waves(level_taps[:, 1], side)
    xr, xi = tap_waves(level_taps[:, 2], side)
    z = level_taps[:, 0].T[:, :, None]
    left = jnp.concatenate(
        [jnp.concatenate([z * yr, -z * yi], 1), jnp.concatenate([z * yi, z * yr], 1)], 2
    )
    return left, jnp.concatenate([xr, xi], 0)


def kernel_modes(level_taps, side):
    left, right = kernel_waves(level_taps, side)
    return jnp.einsum("tmk,mx->tkx", left, right, precision=lax.Precision.HIGHEST)


def row_modes(level_taps, side, row, width):
    left, right = kernel_waves(level_taps, side)
    left = jnp.stack(
        [lax.dynamic_slice_in_dim(left, row, 1, 2)[:, :, 0], lax.dynamic_slice_in_dim(left, side + row, 1, 2)[:, :, 0]], 1
    )
    both = jnp.einsum("tpm,mx->ptx", left, right, precision=lax.Precision.HIGHEST)
    real, imag = both[0], both[1]
    pad = jnp.zeros((TAPS, 64 - 2 * width), F32)
    a = jnp.concatenate([real, real, pad] * 2, 1)
    b = jnp.concatenate([-imag, imag, pad] * 2, 1)
    return a, b


def body(charges, kernel_taps):
    mats = [jnp.asarray(m) for m in dft_parts()]
    me = lax.axis_index("space")

    pieces = []
    for first, layers in CHUNKS + ((7, 1),):
        pieces += forward(charges, first, layers, mats)

    up, down, own, payload = partial_sums(pieces)
    from_below = shifted(up, 1)
    from_above = shifted(down, -1)
    received = lax.all_to_all(payload, "space", 0, 0, tiled=True)

    halos = []
    for k in range(len(CHUNKS)):
        halos.append((shifted(pieces[2 * k + 1], 1), shifted(pieces[2 * k], -1)))

    w0 = kernel_modes(kernel_taps[0], SIDE).reshape(TAPS, 2, SIDE, SIDE)
    w1 = kernel_modes(kernel_taps[1], 64)
    w1 = jnp.concatenate([w1, w1], 2)
    a2, b2 = row_modes(kernel_taps[2], 32, me, 32)
    a3, b3 = row_modes(kernel_taps[3], 16, me % 16, 16)
    spread2 = symbol(32).astype(np.float32)
    spread2 = jnp.asarray(np.tile(spread2, 4)[None, :]) * jnp.asarray(spread2)[me]

    own = jnp.concatenate([own[:2] + from_below, own[2:7], own[7:] + from_above], 0)
    below = shifted(own[:8], 1)
    above = shifted(own[1:], -1)

    spread_out = along_z(received.reshape(COUNT * 16, SIDE), (a2, b2, a3, b3, spread2))
    potentials = lax.all_to_all(spread_out.reshape(COUNT, 16, SIDE), "space", 0, 0, tiled=True)

    acc = local_sums(pieces, w0)
    coarse = level_one(below, own, above, w1, potentials)

    result = finish(4, 4, acc, False, CHUNKS[:1], halos[:1], w0, coarse, mats, None)
    result = finish(2, 2, acc, False, CHUNKS[:2], halos[:2], w0, coarse, mats, result)
    last = finish(0, 2, acc, False, CHUNKS[:2], halos[:2], w0, coarse, None, None)
    return finish(0, 2, last, True, CHUNKS[2:], halos[2:], w0, None, mats, result)


def solution(mesh):
    placed = (P("bead", "space", None, None), P())
    return jax.shard_map(
        body, mesh=mesh, in_specs=placed, out_specs=P("bead", "space", None, None), check_vma=False
    )
```

```python
import functools

import jax
import jax.numpy as jnp
import ml_dtypes
import numpy as np
from jax import lax
from jax.experimental import pallas as pl
from jax.experimental.pallas import tpu as pltpu
from jax.sharding import PartitionSpec as P

REACH = 7
TAPS = 15
SIDE = 128
SLAB = 16
COUNT = 32
F32 = jnp.float32
BF16 = jnp.bfloat16
CUBIC = {0: 1.0, 1: 0.5625, -1: 0.5625, 3: -0.0625, -3: -0.0625}


def symbol(side):
    theta = 2.0 * np.pi * np.arange(side) / side
    return 1.0 + 1.125 * np.cos(theta) - 0.125 * np.cos(3.0 * theta)


def split_const(matrix):
    high = matrix.astype(ml_dtypes.bfloat16)
    low = (matrix - high.astype(np.float64)).astype(ml_dtypes.bfloat16)
    return high, low


def dft_parts():
    angle = 2.0 * np.pi * (np.outer(np.arange(SIDE), np.arange(SIDE)) % SIDE) / SIDE
    c, s = np.cos(angle), np.sin(angle)
    fwd_x = np.block([[c, -s], [s, c]])
    fwd_y = np.block([[c, s], [-s, c]])
    inv_y = np.block([[c, -s], [s, c]]) / SIDE
    inv_x = np.block([[c, s], [-s, c]]) / SIDE
    return np.stack([part for m in (fwd_x, fwd_y, inv_y, inv_x) for part in split_const(m)])


def coarse_parts():
    restrict = np.zeros((64, SIDE))
    for j in range(64):
        for d, weight in CUBIC.items():
            restrict[j, (2 * j + d) % SIDE] += 0.5 * weight
    angle = 2.0 * np.pi * (np.outer(np.arange(64), np.arange(64)) % 64) / 64
    real, imag = np.cos(angle) @ restrict, -np.sin(angle) @ restrict
    along_x = np.block([[real.T, imag.T], [-imag.T, real.T]])
    along_y = np.block([[real, -imag], [imag, real]])
    xh, xl = split_const(along_x)
    yh, yl = split_const(along_y)
    return np.concatenate([np.concatenate([xh, xl], 1), yh, yl], 0)


def fold_weights():
    half = np.outer(symbol(64), symbol(64)) / 16.0
    quarter = np.outer(symbol(32), symbol(32)) / 16.0
    half = np.tile(half, (1, 2))
    quarter = np.concatenate([quarter, quarter * 0, quarter, quarter * 0], axis=1)
    return np.concatenate([half, quarter], 0).astype(np.float32)


def spread_weights():
    full = np.outer(symbol(128), symbol(128))
    half = np.tile(np.outer(symbol(64), symbol(64)), (1, 2))
    return full.astype(np.float32), half.astype(np.float32)


def split(value):
    high = value.astype(BF16)
    return high, (value - high.astype(F32)).astype(BF16)


def dot(a, b):
    return jnp.dot(a, b, preferred_element_type=F32)


def right_mul(value, high, low):
    vh, vl = split(value)
    return dot(vh, high) + dot(vl, high) + dot(vh, low)


def left_mul(high, low, value):
    vh, vl = split(value)
    return dot(high, vh) + dot(high, vl) + dot(low, vh)


def params(megabytes=16):
    return pltpu.CompilerParams(vmem_limit_bytes=megabytes * 1024 * 1024)


def whole(shape):
    return pl.BlockSpec(shape, lambda *_: (0,) * len(shape))


def forward_layer(v, mats, out):
    rows = jnp.concatenate(
        [jnp.concatenate([v[0, 0], v[1, 0]], 1), jnp.concatenate([v[2, 0], v[3, 0]], 1)], 0
    )
    a = right_mul(rows, mats[0], mats[1])
    b = jnp.concatenate(
        [
            jnp.concatenate([a[:SIDE, :SIDE], a[:SIDE, SIDE:]], 0),
            jnp.concatenate([a[SIDE:, :SIDE], a[SIDE:, SIDE:]], 0),
        ],
        1,
    )
    c = left_mul(mats[2], mats[3], b)
    out[0, 0, 0] = c[:SIDE, :SIDE]
    out[0, 0, 1] = c[SIDE:, :SIDE]
    out[0, 1, 0] = c[:SIDE, SIDE:]
    out[0, 1, 1] = c[SIDE:, SIDE:]


def near_kernel(v_low, v_high, mats, own, from_below, from_above, token, out_low, out_high):
    step = pl.program_id(0)

    @pl.when(step < 3)
    def _():
        forward_layer(v_low, mats, out_low)
        forward_layer(v_high, mats, out_high)

    cells = [own[0] + from_below[0], own[1] + from_below[1]] + [own[c] for c in range(2, 7)]
    cells += [own[7] + from_above[0], own[8] + from_above[1]]
    for half in range(2):
        @pl.when(step == 3 + half)
        def _():
            for c in range(4):
                out_high[0, c // 2, c % 2] = cells[4 * half + c]
                out_low[0, c // 2, c % 2] = cells[4 * half + c + 1]


def near_layers(charges, mats, own, from_below, from_above, token):
    shape = jax.ShapeDtypeStruct((5, 2, 2, SIDE, SIDE), F32)
    block = pl.BlockSpec((1, 2, 2, SIDE, SIDE), lambda i: (i, 0, 0, 0, 0))
    return pl.pallas_call(
        near_kernel,
        grid=(5,),
        in_specs=[
            pl.BlockSpec((4, 1, SIDE, SIDE), lambda i: (0, jnp.minimum(i, 2), 0, 0)),
            pl.BlockSpec((4, 1, SIDE, SIDE), lambda i: (0, 13 + jnp.minimum(i, 2), 0, 0)),
            pl.BlockSpec((4, 256, 256), lambda i: (0, 0, 0)),
            whole((9, SIDE, SIDE)),
            whole((2, SIDE, SIDE)),
            whole((2, SIDE, SIDE)),
            pl.BlockSpec(memory_space=pl.ANY),
        ],
        out_specs=[block, block],
        out_shape=[shape, shape],
        compiler_params=params(),
        name="near",
        cost_estimate=pl.CostEstimate(flops=1200000000, bytes_accessed=5000000, transcendentals=0),
    )(charges, charges, mats, own, from_below, from_above, token)


def far_kernel(v_low, v_high, mats, token, out_low, out_high, mid_low, mid_high):
    step = pl.program_id(0)

    @pl.when(step < 4)
    def _():
        forward_layer(v_low, mats, out_low)
        forward_layer(v_high, mats, out_high)

    @pl.when(step == 4)
    def _():
        forward_layer(v_low, mats, mid_low)
        forward_layer(v_high, mats, mid_high)


def far_layers(charges, mats, token):
    shape = jax.ShapeDtypeStruct((4, 2, 2, SIDE, SIDE), F32)
    single = jax.ShapeDtypeStruct((1, 2, 2, SIDE, SIDE), F32)
    block = pl.BlockSpec((1, 2, 2, SIDE, SIDE), lambda i: (jnp.minimum(i, 3), 0, 0, 0, 0))
    fixed = pl.BlockSpec((1, 2, 2, SIDE, SIDE), lambda i: (0, 0, 0, 0, 0))
    return pl.pallas_call(
        far_kernel,
        grid=(5,),
        in_specs=[
            pl.BlockSpec((4, 1, SIDE, SIDE), lambda i: (0, 3 + i, 0, 0)),
            pl.BlockSpec((4, 1, SIDE, SIDE), lambda i: (0, jnp.where(i < 4, 9 + i, 8), 0, 0)),
            pl.BlockSpec((4, 256, 256), lambda i: (0, 0, 0)),
            pl.BlockSpec(memory_space=pl.ANY),
        ],
        out_specs=[block, block, fixed, fixed],
        out_shape=[shape, shape, single, single],
        compiler_params=params(),
        name="far",
        cost_estimate=pl.CostEstimate(flops=2000000000, bytes_accessed=6000000, transcendentals=0),
    )(charges, charges, mats, token)


def fold_lanes(value, lanes):
    return value + pltpu.roll(value, SIDE - lanes, 1)


def restrict_layers(layers, first, low, high):
    out = []
    for cell in range(low, high):
        total = None
        for d, weight in CUBIC.items():
            z = 2 * cell + d - first
            if 0 <= z < len(layers):
                term = (0.5 * weight) * layers[z]
                total = term if total is None else total + term
        out.append(total)
    return out


def partial_kernel(v_hbm, mats, weights, up_ref, down_ref, own_ref, pay_ref, v_ref, mid_ref, sems):
    def copy(k):
        layers = pl.ds(2 * k, 2)
        return pltpu.make_async_copy(v_hbm.at[:, layers], v_ref.at[:, layers], sems.at[k])

    for k in range(SLAB // 2):
        copy(k).start()
    arrived = 0
    lane = lax.broadcasted_iota(jnp.int32, (SIDE, SIDE), 1)
    half, quarter = weights[:64], weights[64:]
    for c in range(-1, 10):
        while arrived < min(SLAB // 2, (2 * c + 3) // 2 + 1):
            copy(arrived).wait()
            arrived += 1
        beads = []
        for bead in range(4):
            total = None
            for d, weight in CUBIC.items():
                z = 2 * c + d
                if 0 <= z < SLAB:
                    term = (0.5 * weight) * v_ref[bead, z]
                    total = term if total is None else total + term
            beads.append(total)
        rows = jnp.concatenate([jnp.concatenate(beads[:2], 1), jnp.concatenate(beads[2:], 1)], 0)
        a = right_mul(rows, mats[:256, :SIDE], mats[:256, SIDE:])
        first, second = a[:SIDE], a[SIDE:]
        real = jnp.where(lane < 64, first, pltpu.roll(second, 64, 1))
        imag = jnp.where(lane < 64, pltpu.roll(first, 64, 1), second)
        value = left_mul(mats[256:384], mats[384:], jnp.concatenate([real, imag], 0))
        mid_ref[c + 1] = value
        if 0 <= c <= 8:
            own_ref[c] = value
        if c in (8, 9):
            up_ref[c - 8] = value
        if c in (-1, 0):
            down_ref[c + 1] = value

    small = []
    for c in range(11):
        parts = []
        for part in range(2):
            g = half * mid_ref[c, 64 * part : 64 * part + 64]
            parts.append(fold_lanes(g[:32] + g[32:], 32))
        small.append(jnp.concatenate(parts, 0))
    level2 = restrict_layers(small, -1, -2, 7)
    lane = lax.broadcasted_iota(jnp.int32, (32, SIDE), 1)
    for c, value in enumerate(level2):
        packed = jnp.where((lane // 32) % 2 == 0, value[:32], pltpu.roll(value[32:], 32, 1))
        pay_ref[:, c, :] = packed

    tiny = []
    for value in level2:
        parts = []
        for part in range(2):
            g = quarter * value[32 * part : 32 * part + 32]
            parts.append(fold_lanes(g[:16] + g[16:], 16))
        tiny.append(jnp.concatenate(parts, 0))
    level3 = restrict_layers(tiny, -2, -2, 5)
    lane = lax.broadcasted_iota(jnp.int32, (16, SIDE), 1)
    for c, value in enumerate(level3):
        packed = jnp.where((lane // 16) % 2 == 0, value[:16], pltpu.roll(value[16:], 16, 1))
        pay_ref[:, 9 + c, :] = jnp.concatenate([packed, packed], 0)


def partial_sums(charges):
    outs = [(2, SIDE, SIDE), (2, SIDE, SIDE), (9, SIDE, SIDE), (COUNT, 16, SIDE)]
    return pl.pallas_call(
        partial_kernel,
        out_shape=[jax.ShapeDtypeStruct(s, F32) for s in outs],
        in_specs=[
            pl.BlockSpec(memory_space=pltpu.HBM),
            pl.BlockSpec(memory_space=pltpu.VMEM),
            pl.BlockSpec(memory_space=pltpu.VMEM),
        ],
        scratch_shapes=[
            pltpu.VMEM((4, SLAB, SIDE, SIDE), F32),
            pltpu.VMEM((11, SIDE, SIDE), F32),
            pltpu.SemaphoreType.DMA((SLAB // 2,)),
        ],
        compiler_params=params(),
        name="partial",
        cost_estimate=pl.CostEstimate(flops=500000000, bytes_accessed=6000000, transcendentals=0),
    )(charges, jnp.asarray(coarse_parts()), jnp.asarray(fold_weights()))


def gather_matrix():
    def places(rows, period, shift, low, high):
        r = lax.broadcasted_iota(jnp.int32, (rows, COUNT * 16), 0)
        q = lax.broadcasted_iota(jnp.int32, (rows, COUNT * 16), 1)
        c = q % 16
        z = (period // COUNT) * (q // 16) + c - low - 2
        hit = ((r - REACH - z) % period == 0) & (c >= low) & (c < high) & (r < period + 2 * REACH)
        return jnp.where(hit, 1.0, 0.0)

    return jnp.concatenate([places(144, 128, 0, 0, 9), places(80, 64, 0, 9, 16)], 0).astype(BF16)


def scatter_matrix():
    r = lax.broadcasted_iota(jnp.int32, (COUNT * 16, 256), 0)
    q = lax.broadcasted_iota(jnp.int32, (COUNT * 16, 256), 1)
    z = 4 * (r // 16) + r % 16 - 2
    same = (z - q) % 128 == 0
    d = jnp.abs((z - 2 * (q - 128) + 64) % 128 - 64)
    weight = jnp.where(d == 0, 1.0, jnp.where(d == 1, 0.5625, jnp.where(d == 3, -0.0625, 0.0)))
    value = jnp.where(q < 128, jnp.where(same, 1.0, 0.0), jnp.where(q < 192, weight, 0.0))
    return jnp.where(r % 16 < 9, value, 0.0).astype(BF16)


def swap_lanes(value, lanes):
    lane = lax.broadcasted_iota(jnp.int32, value.shape, 1)
    return jnp.where((lane // lanes) % 2 == 0, pltpu.roll(value, SIDE - lanes, 1), pltpu.roll(value, lanes, 1))


def along_kernel(x_ref, coefs, out_ref, c_ref, s_ref):
    gather, scatter = gather_matrix(), scatter_matrix()
    a2, b2, a3, b3 = (coefs.at[pl.ds(16 * k, 16)] for k in range(4))
    spread = coefs[64:65]
    xh, xl = split(x_ref[...])
    c_ref[...] = dot(gather, xh) + dot(gather, xl)
    s_ref[:144] = swap_lanes(c_ref[:144], 32)
    s_ref[144:] = swap_lanes(c_ref[144:], 16)
    p2 = jnp.zeros((128, SIDE), F32)
    p3 = jnp.zeros((64, SIDE), F32)
    for t in range(TAPS):
        p2 = p2 + a2[t : t + 1] * c_ref[t : t + 128] + b2[t : t + 1] * s_ref[t : t + 128]
        p3 = p3 + a3[t : t + 1] * c_ref[144 + t : 208 + t] + b3[t : t + 1] * s_ref[144 + t : 208 + t]
    block = (lax.broadcasted_iota(jnp.int32, p3.shape, 1) // 16) % 4
    wide = jnp.where(block == 0, p3, jnp.where(block == 3, pltpu.roll(p3, 32, 1), pltpu.roll(p3, 16, 1)))
    wide = spread * wide
    both = jnp.concatenate([p2, wide, jnp.zeros((64, SIDE), F32)], 0)
    bh, bl = split(both)
    out_ref[...] = dot(scatter, bh) + dot(scatter, bl)


def along_z(received, coefs):
    return pl.pallas_call(
        along_kernel,
        out_shape=jax.ShapeDtypeStruct((COUNT * 16, SIDE), F32),
        scratch_shapes=[pltpu.VMEM((224, SIDE), F32), pltpu.VMEM((224, SIDE), F32)],
        compiler_params=params(),
        name="along",
        cost_estimate=pl.CostEstimate(flops=30000000, bytes_accessed=2000000, transcendentals=0),
    )(received, coefs)


def level_kernel(below, own, last, above, w_ref, p_ref):
    def cell_ref(c):
        ref, c = (below, c + 8) if c < 0 else (own, c) if c < 8 else (last, 7) if c == 8 else (above, c - 9)
        return ref, (3 + c // 4, c // 2 % 2, c % 2)

    def block(r, carry):
        rows = pl.ds(pl.multiple_of(8 * r, 8), 8)
        lower = pl.ds(pl.multiple_of(64 + 8 * r, 8), 8)
        for first, outputs in ((-1, 6), (5, 5)):
            def value(j):
                ref, i = cell_ref(first + j - REACH)
                return ref[(*i, rows)], ref[(*i, lower)]

            sums = slide(outputs, 1, value, lambda t: (w_ref[t, rows], w_ref[t, lower]))
            for i in range(outputs):
                p_ref[first + i + 1, rows] = sums[i][0]
                p_ref[first + i + 1, lower] = sums[i][1]
        return carry

    lax.fori_loop(0, 8, block, 0)


def level_one(below, own, last, above, w1):
    return pl.pallas_call(
        level_kernel,
        out_shape=jax.ShapeDtypeStruct((11, SIDE, SIDE), F32),
        compiler_params=params(),
        name="level",
        cost_estimate=pl.CostEstimate(flops=40000000, bytes_accessed=3000000, transcendentals=0),
    )(below, own, last, above, w1)


def spread_levels(level, y_ref, spread, out_ref, p_ref):
    lane = lax.broadcasted_iota(jnp.int32, (32, SIDE), 1)
    low = (lane // 32) % 2 == 0
    wides = []
    for c in range(9):
        y = y_ref[:, c, :]
        re = jnp.where(low, y, pltpu.roll(y, 32, 1))
        im = jnp.where(low, pltpu.roll(y, SIDE - 32, 1), y)
        wides.append((re, im))
    for c in range(-1, 10):
        for part in range(2):
            total = None
            for d, weight in CUBIC.items():
                if (c - d) % 2 == 0 and -2 <= (c - d) // 2 <= 6:
                    term = weight * wides[(c - d) // 2 + 2][part]
                    total = term if total is None else total + term
            for tile in range(2):
                rows = slice(64 * part + 32 * tile, 64 * part + 32 * tile + 32)
                p_ref[c + 1, rows] = level[c + 1, rows] + spread[32 * tile : 32 * tile + 32] * total
    for z in range(SLAB):
        total = None
        for d, weight in CUBIC.items():
            if (z - d) % 2 == 0:
                term = weight * p_ref[(z - d) // 2 + 1]
                total = term if total is None else total + term
        out_ref[z] = total


def sums_kernel(layers, groups, *refs):
    sources, w_ref, out = refs[:-2], refs[-2], refs[-1]
    for k, z in enumerate(groups):
        def block(r, carry):
            rows = pl.ds(pl.multiple_of(8 * r, 8), 8)

            def value(j):
                if z + j - REACH not in layers:
                    return None
                n, i = layers[z + j - REACH]
                return [sources[n][i, pair, part, rows] for pair in range(2) for part in range(2)]

            sums = slide(4, 2, value, lambda t: (w_ref[t, 0, rows], w_ref[t, 1, rows]))
            for i in range(4):
                for n in range(4):
                    out[4 * k + i, n // 2, n % 2, rows] = sums[i][n]
            return carry

        lax.fori_loop(0, SIDE // 8, block, 0)


def sums_along_z(pieces, layers, groups, w0):
    return pl.pallas_call(
        functools.partial(sums_kernel, layers, groups),
        out_shape=jax.ShapeDtypeStruct((4 * len(groups), 2, 2, SIDE, SIDE), F32),
        compiler_params=params(24),
        name="sums",
        cost_estimate=pl.CostEstimate(flops=100000000, bytes_accessed=9000000, transcendentals=0),
    )(*pieces, w0)


def finish_kernel(
    acc, near_low, near_high, far_low, far_high, w_ref, level, y_ref, small, spread, mats, out, coarse, p_ref, sum_ref
):
    step = pl.program_id(0)

    @pl.when(step == 0)
    def _():
        spread_levels(level, y_ref, small, coarse, p_ref)

    halo = [(far_low, k, k - 7) for k in range(4)] + [(near_low, k, k - 3) for k in range(3)]
    halo += [(near_high, k, 16 + k) for k in range(3)] + [(far_high, k, 19 + k) for k in range(4)]

    def add_halo(first):
        def block(r, carry):
            rows = pl.ds(pl.multiple_of(8 * r, 8), 8)
            for i in range(2):
                sums = [acc[i, pair, part, rows] for pair in range(2) for part in range(2)]
                for ref, k, z in halo:
                    t = z - first - i + REACH
                    if not 0 <= t < TAPS:
                        continue
                    wr, wi = w_ref[t, 0, rows], w_ref[t, 1, rows]
                    for pair in range(2):
                        vr, vi = ref[k, pair, 0, rows], ref[k, pair, 1, rows]
                        sums[2 * pair] += wr * vr - wi * vi
                        sums[2 * pair + 1] += wr * vi + wi * vr
                for n in range(4):
                    sum_ref[i, n // 2, n % 2, rows] = sums[n]
            return carry

        lax.fori_loop(0, SIDE // 8, block, 0)

    for number, first in enumerate((4, 6, 8, 10, 0, 2, 12, 14)):
        @pl.when(step == number)
        def _():
            add_halo(first)

    lane = lax.broadcasted_iota(jnp.int32, (64, SIDE), 1)
    z = 2 * pair_of_layers(step)

    columns = []
    for i in range(2):
        sides = [[], []]
        for part in range(2):
            g = coarse[z + i, 64 * part : 64 * part + 64]
            h = pltpu.roll(g, 64, 1)
            for pair in range(2):
                tile = jnp.where((lane < 64) == (pair == 0), g, h)
                for row in (0, 64):
                    sides[pair].append(sum_ref[i, pair, part, row : row + 64] + spread[row : row + 64] * tile)
        columns += [jnp.concatenate(side, 0) for side in sides]
    c = left_mul(mats[0], mats[1], jnp.concatenate(columns, 1))
    rows = jnp.concatenate(
        [
            jnp.concatenate([c[:SIDE, SIDE * n : SIDE * n + SIDE], c[SIDE:, SIDE * n : SIDE * n + SIDE]], 1)
            for n in range(4)
        ],
        0,
    )
    d = right_mul(rows, mats[2], mats[3])
    for n in range(4):
        for half in range(2):
            out[2 * (n % 2) + half, n // 2] = d[SIDE * n : SIDE * n + SIDE, SIDE * half : SIDE * half + SIDE]


def pair_of_layers(step):
    return jnp.where(step < 4, 2 + step, jnp.where(step < 6, step - 4, step))


def finish(acc, halos, w0, level, potentials, mats):
    full, half = spread_weights()
    return pl.pallas_call(
        finish_kernel,
        grid=(8,),
        in_specs=[
            pl.BlockSpec((2, 2, 2, SIDE, SIDE), lambda i: (pair_of_layers(i), 0, 0, 0, 0)),
            whole((5, 2, 2, SIDE, SIDE)),
            whole((5, 2, 2, SIDE, SIDE)),
            whole((4, 2, 2, SIDE, SIDE)),
            whole((4, 2, 2, SIDE, SIDE)),
            whole((TAPS, 2, SIDE, SIDE)),
            whole((11, SIDE, SIDE)),
            whole((COUNT, 16, SIDE)),
            whole((64, SIDE)),
            whole((SIDE, SIDE)),
            pl.BlockSpec((4, 256, 256), lambda i: (1, 0, 0)),
        ],
        out_specs=pl.BlockSpec((4, 2, SIDE, SIDE), lambda i: (0, pair_of_layers(i), 0, 0)),
        out_shape=jax.ShapeDtypeStruct((4, SLAB, SIDE, SIDE), F32),
        scratch_shapes=[
            pltpu.VMEM((SLAB, SIDE, SIDE), F32),
            pltpu.VMEM((11, SIDE, SIDE), F32),
            pltpu.VMEM((2, 2, 2, SIDE, SIDE), F32),
        ],
        compiler_params=params(28),
        name="finish",
        cost_estimate=pl.CostEstimate(flops=3000000000, bytes_accessed=10000000, transcendentals=0),
    )(acc, *halos, w0, level, potentials, jnp.asarray(half), jnp.asarray(full), mats)


def slide(outputs, pairs, value, weight):
    sums = [[None] * (2 * pairs) for _ in range(outputs)]
    window = {}
    for j in range(outputs + TAPS - 1):
        if j < TAPS:
            window[j] = weight(j)
        v = value(j)
        for i in range(outputs if v is not None else 0):
            t = j - i
            if not 0 <= t < TAPS:
                continue
            wr, wi = window[t]
            for pair in range(pairs):
                vr, vi = v[2 * pair], v[2 * pair + 1]
                for k, term in ((2 * pair, wr * vr - wi * vi), (2 * pair + 1, wr * vi + wi * vr)):
                    sums[i][k] = term if sums[i][k] is None else sums[i][k] + term
    return sums


def shifted(value, steps):
    pairs = [(source, (source + steps) % COUNT) for source in range(COUNT)]
    return lax.ppermute(value, "space", pairs)


def wave_table():
    columns = []
    for side in (128, 64, 32, 16):
        offset = np.arange(SIDE) % max(side, 64)
        lanes = np.where(offset < 2 * side, offset % side, -1)
        angle = 2.0 * np.pi * np.outer(np.arange(TAPS) - REACH, lanes) / side
        columns += [np.where(lanes >= 0, np.cos(angle), 0.0), np.where(lanes >= 0, np.sin(angle), 0.0)]
    return np.concatenate(columns, 1).astype(np.float32)


def modes_kernel(me_ref, taps_ref, rows_ref, cols_ref, z_ref, w0_ref, w1_ref, coef_ref):
    def row(level, term, dim, part):
        return rows_ref[pl.ds((level * 4 + term) * 3 + dim, 1), pl.ds((2 * level + part) * SIDE, SIDE)]

    for level, w_ref, side in ((0, w0_ref, 128), (1, w1_ref, 64)):
        for block in range(0, side, 32):
            real, imag = [], []
            for term in range(4):
                column = (level * 4 + term) * 3 + 1
                yr = cols_ref[pl.ds(2 * level * SIDE + block, 32), pl.ds(column, 1)]
                yi = cols_ref[pl.ds((2 * level + 1) * SIDE + block, 32), pl.ds(column, 1)]
                xr, xi = row(level, term, 2, 0), row(level, term, 2, 1)
                real.append(yr * xr - yi * xi)
                imag.append(yr * xi + yi * xr)

            def tap(t, carry):
                for part, values in ((0, real), (1, imag)):
                    total = None
                    for term in range(4):
                        scaled = taps_ref[(level * 4 + term) * TAPS + t] * values[term]
                        total = scaled if total is None else total + scaled
                    w_ref[t, pl.ds(part * side + block, 32)] = total
                return carry

            lax.fori_loop(0, TAPS, tap, 0)

    me = me_ref[0]
    coef_ref[...] = jnp.zeros_like(coef_ref)
    for level, base, side in ((2, 0, 32), (3, 32, 16)):
        lane = lax.broadcasted_iota(jnp.int32, (1, SIDE), 1)
        sign = jnp.where((lane // side) % 2 == 0, -1.0, 1.0)
        chosen = lane == lax.rem(me, side)
        a = b = None
        for term in range(4):
            yr = jnp.sum(jnp.where(chosen, row(level, term, 1, 0), 0.0), axis=1, keepdims=True)
            yi = jnp.sum(jnp.where(chosen, row(level, term, 1, 1), 0.0), axis=1, keepdims=True)
            xr, xi = row(level, term, 2, 0), row(level, term, 2, 1)
            z = z_ref[:, pl.ds(level * 4 + term, 1)]
            ta = z * (yr * xr - yi * xi)
            tb = z * (sign * (yr * xi + yi * xr))
            a = ta if a is None else a + ta
            b = tb if b is None else b + tb
        coef_ref[pl.ds(base, TAPS)] = a
        coef_ref[pl.ds(base + 16, TAPS)] = b
    lane = lax.broadcasted_iota(jnp.int32, (1, SIDE), 1)
    theta = (lane % 32).astype(F32) * (2.0 * np.pi / 32)
    symbols = 1.0 + 1.125 * jnp.cos(theta) - 0.125 * jnp.cos(3.0 * theta)
    chosen = jnp.sum(jnp.where(lane == me, symbols, 0.0), axis=1, keepdims=True)
    coef_ref[pl.ds(64, 1)] = symbols * chosen


def kernel_modes(taps, me):
    table = jnp.asarray(wave_table())
    flat = taps.reshape(48, TAPS)
    z = taps[:, :, 0].reshape(16, TAPS)
    exact = lax.Precision.HIGHEST
    rows = jnp.dot(flat, table, precision=exact)
    cols = jnp.dot(jnp.asarray(wave_table().T), flat.T, precision=exact)
    outs = [(TAPS, 256, SIDE), (TAPS, SIDE, SIDE), (80, SIDE)]
    in_smem = pl.BlockSpec(memory_space=pltpu.SMEM)
    in_vmem = pl.BlockSpec(memory_space=pltpu.VMEM)
    return pl.pallas_call(
        modes_kernel,
        in_specs=[in_smem, in_smem, in_vmem, in_vmem, in_vmem],
        out_shape=[jax.ShapeDtypeStruct(s, F32) for s in outs],
        compiler_params=params(),
        name="modes",
        cost_estimate=pl.CostEstimate(flops=8000000, bytes_accessed=4000000, transcendentals=0),
    )(me.reshape(1), z.reshape(-1), rows, cols, z.T)


def body(charges, kernel_taps):
    mats = jnp.asarray(dft_parts())
    charges = pltpu.with_memory_space_constraint(charges, pltpu.HBM)
    me = lax.axis_index("space")

    to_above, to_below, own, payload = partial_sums(charges)
    from_below = shifted(to_above, 1)
    from_above = shifted(to_below, -1)
    received = lax.all_to_all(payload, "space", 0, 0, tiled=True)

    near_down, near_up = near_layers(charges, mats, own, from_below, from_above, own)
    near_lower, near_upper = shifted(near_up, 1), shifted(near_down, -1)
    far_down, far_up, low_mid, high_mid = far_layers(charges, mats, near_up)
    far_lower, far_upper = shifted(far_up, 1), shifted(far_down, -1)

    w0, w1, coefs = kernel_modes(kernel_taps, me)
    w0 = w0.reshape(TAPS, 2, SIDE, SIDE)

    spread_out = along_z(received.reshape(COUNT * 16, SIDE), coefs)
    potentials = lax.all_to_all(spread_out.reshape(COUNT, 16, SIDE), "space", 0, 0, tiled=True)

    pieces = (near_down, far_down, low_mid, high_mid, far_up, near_up)
    places = ((0, 3), (3, 4), (7, 1), (8, 1), (9, 4), (13, 3))
    layers = {first + i: (k, i) for k, (first, count) in enumerate(places) for i in range(count)}
    acc = sums_along_z(pieces, layers, (0, 4, 8, 12), w0)
    acc = pltpu.with_memory_space_constraint(acc, pltpu.HBM)
    level = level_one(near_lower, near_up, near_down, near_upper, w1)
    return finish(acc, (near_lower, near_upper, far_lower, far_upper), w0, level, potentials, mats)


def solution(mesh):
    placed = (P("bead", "space", None, None), P())
    return jax.shard_map(
        body, mesh=mesh, in_specs=placed, out_specs=P("bead", "space", None, None), check_vma=False
    )
```

```python
import functools

import jax
import jax.numpy as jnp
import ml_dtypes
import numpy as np
from jax import lax
from jax.experimental import pallas as pl
from jax.experimental.pallas import tpu as pltpu
from jax.sharding import PartitionSpec as P

REACH = 7
TAPS = 15
SIDE = 128
SLAB = 16
COUNT = 32
F32 = jnp.float32
BF16 = jnp.bfloat16
CUBIC = {0: 1.0, 1: 0.5625, -1: 0.5625, 3: -0.0625, -3: -0.0625}


def symbol(side):
    theta = 2.0 * np.pi * np.arange(side) / side
    return 1.0 + 1.125 * np.cos(theta) - 0.125 * np.cos(3.0 * theta)


def split_const(matrix):
    high = matrix.astype(ml_dtypes.bfloat16)
    low = (matrix - high.astype(np.float64)).astype(ml_dtypes.bfloat16)
    return high, low


def dft_parts():
    angle = 2.0 * np.pi * (np.outer(np.arange(SIDE), np.arange(SIDE)) % SIDE) / SIDE
    c, s = np.cos(angle), np.sin(angle)
    fwd_x = np.block([[c, -s], [s, c]])
    fwd_y = np.block([[c, s], [-s, c]])
    inv_y = np.block([[c, -s], [s, c]]) / SIDE
    inv_x = np.block([[c, s], [-s, c]]) / SIDE
    return np.stack([part for m in (fwd_x, fwd_y, inv_y, inv_x) for part in split_const(m)])


def coarse_parts():
    restrict = np.zeros((64, SIDE))
    for j in range(64):
        for d, weight in CUBIC.items():
            restrict[j, (2 * j + d) % SIDE] += 0.5 * weight
    angle = 2.0 * np.pi * (np.outer(np.arange(64), np.arange(64)) % 64) / 64
    real, imag = np.cos(angle) @ restrict, -np.sin(angle) @ restrict
    along_x = np.block([[real.T, imag.T], [-imag.T, real.T]])
    along_y = np.block([[real, -imag], [imag, real]])
    xh, xl = split_const(along_x)
    yh, yl = split_const(along_y)
    return np.concatenate([np.concatenate([xh, xl], 1), yh, yl], 0)


def fold_weights():
    half = np.outer(symbol(64), symbol(64)) / 16.0
    quarter = np.outer(symbol(32), symbol(32)) / 16.0
    half = np.tile(half, (1, 2))
    quarter = np.concatenate([quarter, quarter * 0, quarter, quarter * 0], axis=1)
    return np.concatenate([half, quarter], 0).astype(np.float32)


def spread_weights():
    full = np.outer(symbol(128), symbol(128))
    half = np.tile(np.outer(symbol(64), symbol(64)), (1, 2))
    return full.astype(np.float32), half.astype(np.float32)


def split(value):
    high = value.astype(BF16)
    return high, (value - high.astype(F32)).astype(BF16)


def dot(a, b):
    return jnp.dot(a, b, preferred_element_type=F32)


def right_mul(value, high, low):
    vh, vl = split(value)
    return dot(vh, high) + dot(vl, high) + dot(vh, low)


def left_mul(high, low, value):
    vh, vl = split(value)
    return dot(high, vh) + dot(high, vl) + dot(low, vh)


def params(megabytes=16):
    return pltpu.CompilerParams(vmem_limit_bytes=megabytes * 1024 * 1024)


def whole(shape):
    return pl.BlockSpec(shape, lambda *_: (0,) * len(shape))


def forward_layer(v, mats, out):
    rows = jnp.concatenate(
        [jnp.concatenate([v[0, 0], v[1, 0]], 1), jnp.concatenate([v[2, 0], v[3, 0]], 1)], 0
    )
    a = right_mul(rows, mats[0], mats[1])
    b = jnp.concatenate(
        [
            jnp.concatenate([a[:SIDE, :SIDE], a[:SIDE, SIDE:]], 0),
            jnp.concatenate([a[SIDE:, :SIDE], a[SIDE:, SIDE:]], 0),
        ],
        1,
    )
    c = left_mul(mats[2], mats[3], b)
    out[0, 0, 0] = c[:SIDE, :SIDE]
    out[0, 0, 1] = c[SIDE:, :SIDE]
    out[0, 1, 0] = c[:SIDE, SIDE:]
    out[0, 1, 1] = c[SIDE:, SIDE:]


def near_kernel(v_low, v_high, mats, own, from_below, from_above, token, out_low, out_high):
    step = pl.program_id(0)

    @pl.when(step < 3)
    def _():
        forward_layer(v_low, mats, out_low)
        forward_layer(v_high, mats, out_high)

    cells = [own[0] + from_below[0], own[1] + from_below[1]] + [own[c] for c in range(2, 7)]
    cells += [own[7] + from_above[0], own[8] + from_above[1]]
    for half in range(2):
        @pl.when(step == 3 + half)
        def _():
            for c in range(4):
                out_high[0, c // 2, c % 2] = cells[4 * half + c]
                out_low[0, c // 2, c % 2] = cells[4 * half + c + 1]


def near_layers(charges, mats, own, from_below, from_above, token):
    shape = jax.ShapeDtypeStruct((5, 2, 2, SIDE, SIDE), F32)
    block = pl.BlockSpec((1, 2, 2, SIDE, SIDE), lambda i: (i, 0, 0, 0, 0))
    return pl.pallas_call(
        near_kernel,
        grid=(5,),
        in_specs=[
            pl.BlockSpec((4, 1, SIDE, SIDE), lambda i: (0, jnp.minimum(i, 2), 0, 0)),
            pl.BlockSpec((4, 1, SIDE, SIDE), lambda i: (0, 13 + jnp.minimum(i, 2), 0, 0)),
            pl.BlockSpec((4, 256, 256), lambda i: (0, 0, 0)),
            whole((9, SIDE, SIDE)),
            whole((2, SIDE, SIDE)),
            whole((2, SIDE, SIDE)),
            pl.BlockSpec(memory_space=pl.ANY),
        ],
        out_specs=[block, block],
        out_shape=[shape, shape],
        compiler_params=params(),
        name="near",
        cost_estimate=pl.CostEstimate(flops=1000, bytes_accessed=1000, transcendentals=0),
    )(charges, charges, mats, own, from_below, from_above, token)


def far_kernel(v_low, v_high, mats, token, out_low, out_high, mid_low, mid_high):
    step = pl.program_id(0)

    @pl.when(step < 4)
    def _():
        forward_layer(v_low, mats, out_low)
        forward_layer(v_high, mats, out_high)

    @pl.when(step == 4)
    def _():
        forward_layer(v_low, mats, mid_low)
        forward_layer(v_high, mats, mid_high)


def far_layers(charges, mats, token):
    shape = jax.ShapeDtypeStruct((4, 2, 2, SIDE, SIDE), F32)
    single = jax.ShapeDtypeStruct((1, 2, 2, SIDE, SIDE), F32)
    block = pl.BlockSpec((1, 2, 2, SIDE, SIDE), lambda i: (jnp.minimum(i, 3), 0, 0, 0, 0))
    fixed = pl.BlockSpec((1, 2, 2, SIDE, SIDE), lambda i: (0, 0, 0, 0, 0))
    return pl.pallas_call(
        far_kernel,
        grid=(5,),
        in_specs=[
            pl.BlockSpec((4, 1, SIDE, SIDE), lambda i: (0, 3 + i, 0, 0)),
            pl.BlockSpec((4, 1, SIDE, SIDE), lambda i: (0, jnp.where(i < 4, 9 + i, 8), 0, 0)),
            pl.BlockSpec((4, 256, 256), lambda i: (0, 0, 0)),
            pl.BlockSpec(memory_space=pl.ANY),
        ],
        out_specs=[block, block, fixed, fixed],
        out_shape=[shape, shape, single, single],
        compiler_params=params(),
        name="far",
        cost_estimate=pl.CostEstimate(flops=1000, bytes_accessed=1000, transcendentals=0),
    )(charges, charges, mats, token)


def fold_lanes(value, lanes):
    return value + pltpu.roll(value, SIDE - lanes, 1)


def restrict_layers(layers, first, low, high):
    out = []
    for cell in range(low, high):
        total = None
        for d, weight in CUBIC.items():
            z = 2 * cell + d - first
            if 0 <= z < len(layers):
                term = (0.5 * weight) * layers[z]
                total = term if total is None else total + term
        out.append(total)
    return out


def partial_kernel(v_hbm, mats, weights, up_ref, down_ref, own_ref, pay_ref, v_ref, mid_ref, sems):
    def copy(k):
        layers = pl.ds(2 * k, 2)
        return pltpu.make_async_copy(v_hbm.at[:, layers], v_ref.at[:, layers], sems.at[k])

    for k in range(SLAB // 2):
        copy(k).start()
    arrived = 0
    lane = lax.broadcasted_iota(jnp.int32, (SIDE, SIDE), 1)
    half, quarter = weights[:64], weights[64:]
    for c in range(-1, 10):
        while arrived < min(SLAB // 2, (2 * c + 3) // 2 + 1):
            copy(arrived).wait()
            arrived += 1
        beads = []
        for bead in range(4):
            total = None
            for d, weight in CUBIC.items():
                z = 2 * c + d
                if 0 <= z < SLAB:
                    term = (0.5 * weight) * v_ref[bead, z]
                    total = term if total is None else total + term
            beads.append(total)
        rows = jnp.concatenate([jnp.concatenate(beads[:2], 1), jnp.concatenate(beads[2:], 1)], 0)
        a = right_mul(rows, mats[:256, :SIDE], mats[:256, SIDE:])
        first, second = a[:SIDE], a[SIDE:]
        real = jnp.where(lane < 64, first, pltpu.roll(second, 64, 1))
        imag = jnp.where(lane < 64, pltpu.roll(first, 64, 1), second)
        value = left_mul(mats[256:384], mats[384:], jnp.concatenate([real, imag], 0))
        mid_ref[c + 1] = value
        if 0 <= c <= 8:
            own_ref[c] = value
        if c in (8, 9):
            up_ref[c - 8] = value
        if c in (-1, 0):
            down_ref[c + 1] = value

    small = []
    for c in range(11):
        parts = []
        for part in range(2):
            g = half * mid_ref[c, 64 * part : 64 * part + 64]
            parts.append(fold_lanes(g[:32] + g[32:], 32))
        small.append(jnp.concatenate(parts, 0))
    level2 = restrict_layers(small, -1, -2, 7)
    lane = lax.broadcasted_iota(jnp.int32, (32, SIDE), 1)
    for c, value in enumerate(level2):
        packed = jnp.where((lane // 32) % 2 == 0, value[:32], pltpu.roll(value[32:], 32, 1))
        pay_ref[:, c, :] = packed

    tiny = []
    for value in level2:
        parts = []
        for part in range(2):
            g = quarter * value[32 * part : 32 * part + 32]
            parts.append(fold_lanes(g[:16] + g[16:], 16))
        tiny.append(jnp.concatenate(parts, 0))
    level3 = restrict_layers(tiny, -2, -2, 5)
    lane = lax.broadcasted_iota(jnp.int32, (16, SIDE), 1)
    for c, value in enumerate(level3):
        packed = jnp.where((lane // 16) % 2 == 0, value[:16], pltpu.roll(value[16:], 16, 1))
        pay_ref[:, 9 + c, :] = jnp.concatenate([packed, packed], 0)


def partial_sums(charges):
    outs = [(2, SIDE, SIDE), (2, SIDE, SIDE), (9, SIDE, SIDE), (COUNT, 16, SIDE)]
    return pl.pallas_call(
        partial_kernel,
        out_shape=[jax.ShapeDtypeStruct(s, F32) for s in outs],
        in_specs=[
            pl.BlockSpec(memory_space=pltpu.HBM),
            pl.BlockSpec(memory_space=pltpu.VMEM),
            pl.BlockSpec(memory_space=pltpu.VMEM),
        ],
        scratch_shapes=[
            pltpu.VMEM((4, SLAB, SIDE, SIDE), F32),
            pltpu.VMEM((11, SIDE, SIDE), F32),
            pltpu.SemaphoreType.DMA((SLAB // 2,)),
        ],
        compiler_params=params(),
        name="partial",
        cost_estimate=pl.CostEstimate(flops=1000, bytes_accessed=1000, transcendentals=0),
    )(charges, jnp.asarray(coarse_parts()), jnp.asarray(fold_weights()))


def gather_matrix():
    def places(rows, period, shift, low, high):
        r = lax.broadcasted_iota(jnp.int32, (rows, COUNT * 16), 0)
        q = lax.broadcasted_iota(jnp.int32, (rows, COUNT * 16), 1)
        c = q % 16
        z = (period // COUNT) * (q // 16) + c - low - 2
        hit = ((r - REACH - z) % period == 0) & (c >= low) & (c < high) & (r < period + 2 * REACH)
        return jnp.where(hit, 1.0, 0.0)

    return jnp.concatenate([places(144, 128, 0, 0, 9), places(80, 64, 0, 9, 16)], 0).astype(BF16)


def scatter_matrix():
    r = lax.broadcasted_iota(jnp.int32, (COUNT * 16, 256), 0)
    q = lax.broadcasted_iota(jnp.int32, (COUNT * 16, 256), 1)
    z = 4 * (r // 16) + r % 16 - 2
    same = (z - q) % 128 == 0
    d = jnp.abs((z - 2 * (q - 128) + 64) % 128 - 64)
    weight = jnp.where(d == 0, 1.0, jnp.where(d == 1, 0.5625, jnp.where(d == 3, -0.0625, 0.0)))
    value = jnp.where(q < 128, jnp.where(same, 1.0, 0.0), jnp.where(q < 192, weight, 0.0))
    return jnp.where(r % 16 < 9, value, 0.0).astype(BF16)


def swap_lanes(value, lanes):
    lane = lax.broadcasted_iota(jnp.int32, value.shape, 1)
    return jnp.where((lane // lanes) % 2 == 0, pltpu.roll(value, SIDE - lanes, 1), pltpu.roll(value, lanes, 1))


def along_kernel(x_ref, coefs, out_ref, c_ref, s_ref):
    gather, scatter = gather_matrix(), scatter_matrix()
    a2, b2, a3, b3 = (coefs.at[pl.ds(16 * k, 16)] for k in range(4))
    spread = coefs[64:65]
    xh, xl = split(x_ref[...])
    c_ref[...] = dot(gather, xh) + dot(gather, xl)
    s_ref[:144] = swap_lanes(c_ref[:144], 32)
    s_ref[144:] = swap_lanes(c_ref[144:], 16)
    p2 = jnp.zeros((128, SIDE), F32)
    p3 = jnp.zeros((64, SIDE), F32)
    for t in range(TAPS):
        p2 = p2 + a2[t : t + 1] * c_ref[t : t + 128] + b2[t : t + 1] * s_ref[t : t + 128]
        p3 = p3 + a3[t : t + 1] * c_ref[144 + t : 208 + t] + b3[t : t + 1] * s_ref[144 + t : 208 + t]
    block = (lax.broadcasted_iota(jnp.int32, p3.shape, 1) // 16) % 4
    wide = jnp.where(block == 0, p3, jnp.where(block == 3, pltpu.roll(p3, 32, 1), pltpu.roll(p3, 16, 1)))
    wide = spread * wide
    both = jnp.concatenate([p2, wide, jnp.zeros((64, SIDE), F32)], 0)
    bh, bl = split(both)
    out_ref[...] = dot(scatter, bh) + dot(scatter, bl)


def along_z(received, coefs):
    return pl.pallas_call(
        along_kernel,
        out_shape=jax.ShapeDtypeStruct((COUNT * 16, SIDE), F32),
        scratch_shapes=[pltpu.VMEM((224, SIDE), F32), pltpu.VMEM((224, SIDE), F32)],
        compiler_params=params(),
        name="along",
        cost_estimate=pl.CostEstimate(flops=100000000000, bytes_accessed=400000000, transcendentals=0),
    )(received, coefs)


def level_kernel(below, own, last, above, w_ref, p_ref):
    def cell_ref(c):
        ref, c = (below, c + 8) if c < 0 else (own, c) if c < 8 else (last, 7) if c == 8 else (above, c - 9)
        return ref, (3 + c // 4, c // 2 % 2, c % 2)

    def block(r, carry):
        rows = pl.ds(pl.multiple_of(8 * r, 8), 8)
        lower = pl.ds(pl.multiple_of(64 + 8 * r, 8), 8)
        for first, outputs in ((-1, 6), (5, 5)):
            def value(j):
                ref, i = cell_ref(first + j - REACH)
                return ref[(*i, rows)], ref[(*i, lower)]

            sums = slide(outputs, 1, value, lambda t: (w_ref[t, rows], w_ref[t, lower]))
            for i in range(outputs):
                p_ref[first + i + 1, rows] = sums[i][0]
                p_ref[first + i + 1, lower] = sums[i][1]
        return carry

    lax.fori_loop(0, 8, block, 0)


def level_one(below, own, last, above, w1):
    return pl.pallas_call(
        level_kernel,
        out_shape=jax.ShapeDtypeStruct((11, SIDE, SIDE), F32),
        compiler_params=params(),
        name="level",
        cost_estimate=pl.CostEstimate(flops=1000, bytes_accessed=1000, transcendentals=0),
    )(below, own, last, above, w1)


def spread_levels(level, y_ref, spread, out_ref, p_ref):
    lane = lax.broadcasted_iota(jnp.int32, (32, SIDE), 1)
    low = (lane // 32) % 2 == 0
    wides = []
    for c in range(9):
        y = y_ref[:, c, :]
        re = jnp.where(low, y, pltpu.roll(y, 32, 1))
        im = jnp.where(low, pltpu.roll(y, SIDE - 32, 1), y)
        wides.append((re, im))
    for c in range(-1, 10):
        for part in range(2):
            total = None
            for d, weight in CUBIC.items():
                if (c - d) % 2 == 0 and -2 <= (c - d) // 2 <= 6:
                    term = weight * wides[(c - d) // 2 + 2][part]
                    total = term if total is None else total + term
            for tile in range(2):
                rows = slice(64 * part + 32 * tile, 64 * part + 32 * tile + 32)
                p_ref[c + 1, rows] = level[c + 1, rows] + spread[32 * tile : 32 * tile + 32] * total
    for z in range(SLAB):
        total = None
        for d, weight in CUBIC.items():
            if (z - d) % 2 == 0:
                term = weight * p_ref[(z - d) // 2 + 1]
                total = term if total is None else total + term
        out_ref[z] = total


def sums_kernel(layers, groups, *refs):
    sources, w_ref, out = refs[:-2], refs[-2], refs[-1]
    for k, z in enumerate(groups):
        def block(r, carry):
            rows = pl.ds(pl.multiple_of(8 * r, 8), 8)

            def value(j):
                if z + j - REACH not in layers:
                    return None
                n, i = layers[z + j - REACH]
                return [sources[n][i, pair, part, rows] for pair in range(2) for part in range(2)]

            sums = slide(4, 2, value, lambda t: (w_ref[t, 0, rows], w_ref[t, 1, rows]))
            for i in range(4):
                for n in range(4):
                    out[4 * k + i, n // 2, n % 2, rows] = sums[i][n]
            return carry

        lax.fori_loop(0, SIDE // 8, block, 0)


def sums_along_z(pieces, layers, groups, w0):
    return pl.pallas_call(
        functools.partial(sums_kernel, layers, groups),
        out_shape=jax.ShapeDtypeStruct((4 * len(groups), 2, 2, SIDE, SIDE), F32),
        compiler_params=params(24),
        name="sums",
        cost_estimate=pl.CostEstimate(flops=1000, bytes_accessed=1000, transcendentals=0),
    )(*pieces, w0)


def finish_kernel(
    acc, near_low, near_high, far_low, far_high, w_ref, level, y_ref, small, spread, mats, out, coarse, p_ref, sum_ref
):
    step = pl.program_id(0)

    @pl.when(step == 0)
    def _():
        spread_levels(level, y_ref, small, coarse, p_ref)

    halo = [(far_low, k, k - 7) for k in range(4)] + [(near_low, k, k - 3) for k in range(3)]
    halo += [(near_high, k, 16 + k) for k in range(3)] + [(far_high, k, 19 + k) for k in range(4)]

    def add_halo(first):
        def block(r, carry):
            rows = pl.ds(pl.multiple_of(8 * r, 8), 8)
            for i in range(2):
                sums = [acc[i, pair, part, rows] for pair in range(2) for part in range(2)]
                for ref, k, z in halo:
                    t = z - first - i + REACH
                    if not 0 <= t < TAPS:
                        continue
                    wr, wi = w_ref[t, 0, rows], w_ref[t, 1, rows]
                    for pair in range(2):
                        vr, vi = ref[k, pair, 0, rows], ref[k, pair, 1, rows]
                        sums[2 * pair] += wr * vr - wi * vi
                        sums[2 * pair + 1] += wr * vi + wi * vr
                for n in range(4):
                    sum_ref[i, n // 2, n % 2, rows] = sums[n]
            return carry

        lax.fori_loop(0, SIDE // 8, block, 0)

    for number, first in enumerate((4, 6, 8, 10, 0, 2, 12, 14)):
        @pl.when(step == number)
        def _():
            add_halo(first)

    lane = lax.broadcasted_iota(jnp.int32, (64, SIDE), 1)
    z = 2 * pair_of_layers(step)

    columns = []
    for i in range(2):
        sides = [[], []]
        for part in range(2):
            g = coarse[z + i, 64 * part : 64 * part + 64]
            h = pltpu.roll(g, 64, 1)
            for pair in range(2):
                tile = jnp.where((lane < 64) == (pair == 0), g, h)
                for row in (0, 64):
                    sides[pair].append(sum_ref[i, pair, part, row : row + 64] + spread[row : row + 64] * tile)
        columns += [jnp.concatenate(side, 0) for side in sides]
    c = left_mul(mats[0], mats[1], jnp.concatenate(columns, 1))
    rows = jnp.concatenate(
        [
            jnp.concatenate([c[:SIDE, SIDE * n : SIDE * n + SIDE], c[SIDE:, SIDE * n : SIDE * n + SIDE]], 1)
            for n in range(4)
        ],
        0,
    )
    d = right_mul(rows, mats[2], mats[3])
    for n in range(4):
        for half in range(2):
            out[2 * (n % 2) + half, n // 2] = d[SIDE * n : SIDE * n + SIDE, SIDE * half : SIDE * half + SIDE]


def pair_of_layers(step):
    return jnp.where(step < 4, 2 + step, jnp.where(step < 6, step - 4, step))


def finish(acc, halos, w0, level, potentials, mats):
    full, half = spread_weights()
    return pl.pallas_call(
        finish_kernel,
        grid=(8,),
        in_specs=[
            pl.BlockSpec((2, 2, 2, SIDE, SIDE), lambda i: (pair_of_layers(i), 0, 0, 0, 0)),
            whole((5, 2, 2, SIDE, SIDE)),
            whole((5, 2, 2, SIDE, SIDE)),
            whole((4, 2, 2, SIDE, SIDE)),
            whole((4, 2, 2, SIDE, SIDE)),
            whole((TAPS, 2, SIDE, SIDE)),
            whole((11, SIDE, SIDE)),
            whole((COUNT, 16, SIDE)),
            whole((64, SIDE)),
            whole((SIDE, SIDE)),
            pl.BlockSpec((4, 256, 256), lambda i: (1, 0, 0)),
        ],
        out_specs=pl.BlockSpec((4, 2, SIDE, SIDE), lambda i: (0, pair_of_layers(i), 0, 0)),
        out_shape=jax.ShapeDtypeStruct((4, SLAB, SIDE, SIDE), F32),
        scratch_shapes=[
            pltpu.VMEM((SLAB, SIDE, SIDE), F32),
            pltpu.VMEM((11, SIDE, SIDE), F32),
            pltpu.VMEM((2, 2, 2, SIDE, SIDE), F32),
        ],
        compiler_params=params(28),
        name="finish",
        cost_estimate=pl.CostEstimate(flops=1000, bytes_accessed=1000, transcendentals=0),
    )(acc, *halos, w0, level, potentials, jnp.asarray(half), jnp.asarray(full), mats)


def slide(outputs, pairs, value, weight):
    sums = [[None] * (2 * pairs) for _ in range(outputs)]
    window = {}
    for j in range(outputs + TAPS - 1):
        if j < TAPS:
            window[j] = weight(j)
        v = value(j)
        for i in range(outputs if v is not None else 0):
            t = j - i
            if not 0 <= t < TAPS:
                continue
            wr, wi = window[t]
            for pair in range(pairs):
                vr, vi = v[2 * pair], v[2 * pair + 1]
                for k, term in ((2 * pair, wr * vr - wi * vi), (2 * pair + 1, wr * vi + wi * vr)):
                    sums[i][k] = term if sums[i][k] is None else sums[i][k] + term
    return sums


def shifted(value, steps):
    pairs = [(source, (source + steps) % COUNT) for source in range(COUNT)]
    return lax.ppermute(value, "space", pairs)


def wave_table():
    columns = []
    for side in (128, 64, 32, 16):
        offset = np.arange(SIDE) % max(side, 64)
        lanes = np.where(offset < 2 * side, offset % side, -1)
        angle = 2.0 * np.pi * np.outer(np.arange(TAPS) - REACH, lanes) / side
        columns += [np.where(lanes >= 0, np.cos(angle), 0.0), np.where(lanes >= 0, np.sin(angle), 0.0)]
    return np.concatenate(columns, 1).astype(np.float32)


def modes_kernel(me_ref, taps_ref, rows_ref, cols_ref, z_ref, w0_ref, w1_ref, coef_ref):
    def row(level, term, dim, part):
        return rows_ref[pl.ds((level * 4 + term) * 3 + dim, 1), pl.ds((2 * level + part) * SIDE, SIDE)]

    for level, w_ref, side in ((0, w0_ref, 128), (1, w1_ref, 64)):
        for block in range(0, side, 32):
            real, imag = [], []
            for term in range(4):
                column = (level * 4 + term) * 3 + 1
                yr = cols_ref[pl.ds(2 * level * SIDE + block, 32), pl.ds(column, 1)]
                yi = cols_ref[pl.ds((2 * level + 1) * SIDE + block, 32), pl.ds(column, 1)]
                xr, xi = row(level, term, 2, 0), row(level, term, 2, 1)
                real.append(yr * xr - yi * xi)
                imag.append(yr * xi + yi * xr)

            def tap(t, carry):
                for part, values in ((0, real), (1, imag)):
                    total = None
                    for term in range(4):
                        scaled = taps_ref[(level * 4 + term) * TAPS + t] * values[term]
                        total = scaled if total is None else total + scaled
                    w_ref[t, pl.ds(part * side + block, 32)] = total
                return carry

            lax.fori_loop(0, TAPS, tap, 0)

    me = me_ref[0]
    coef_ref[...] = jnp.zeros_like(coef_ref)
    for level, base, side in ((2, 0, 32), (3, 32, 16)):
        lane = lax.broadcasted_iota(jnp.int32, (1, SIDE), 1)
        sign = jnp.where((lane // side) % 2 == 0, -1.0, 1.0)
        chosen = lane == lax.rem(me, side)
        a = b = None
        for term in range(4):
            yr = jnp.sum(jnp.where(chosen, row(level, term, 1, 0), 0.0), axis=1, keepdims=True)
            yi = jnp.sum(jnp.where(chosen, row(level, term, 1, 1), 0.0), axis=1, keepdims=True)
            xr, xi = row(level, term, 2, 0), row(level, term, 2, 1)
            z = z_ref[:, pl.ds(level * 4 + term, 1)]
            ta = z * (yr * xr - yi * xi)
            tb = z * (sign * (yr * xi + yi * xr))
            a = ta if a is None else a + ta
            b = tb if b is None else b + tb
        coef_ref[pl.ds(base, TAPS)] = a
        coef_ref[pl.ds(base + 16, TAPS)] = b
    lane = lax.broadcasted_iota(jnp.int32, (1, SIDE), 1)
    theta = (lane % 32).astype(F32) * (2.0 * np.pi / 32)
    symbols = 1.0 + 1.125 * jnp.cos(theta) - 0.125 * jnp.cos(3.0 * theta)
    chosen = jnp.sum(jnp.where(lane == me, symbols, 0.0), axis=1, keepdims=True)
    coef_ref[pl.ds(64, 1)] = symbols * chosen


def kernel_modes(taps, me):
    table = jnp.asarray(wave_table())
    flat = taps.reshape(48, TAPS)
    z = taps[:, :, 0].reshape(16, TAPS)
    exact = lax.Precision.HIGHEST
    rows = jnp.dot(flat, table, precision=exact)
    cols = jnp.dot(jnp.asarray(wave_table().T), flat.T, precision=exact)
    outs = [(TAPS, 256, SIDE), (TAPS, SIDE, SIDE), (80, SIDE)]
    in_smem = pl.BlockSpec(memory_space=pltpu.SMEM)
    in_vmem = pl.BlockSpec(memory_space=pltpu.VMEM)
    return pl.pallas_call(
        modes_kernel,
        in_specs=[in_smem, in_smem, in_vmem, in_vmem, in_vmem],
        out_shape=[jax.ShapeDtypeStruct(s, F32) for s in outs],
        compiler_params=params(),
        name="modes",
        cost_estimate=pl.CostEstimate(flops=1000, bytes_accessed=1000, transcendentals=0),
    )(me.reshape(1), z.reshape(-1), rows, cols, z.T)


def body(charges, kernel_taps):
    mats = jnp.asarray(dft_parts())
    charges = pltpu.with_memory_space_constraint(charges, pltpu.HBM)
    me = lax.axis_index("space")

    to_above, to_below, own, payload = partial_sums(charges)
    from_below = shifted(to_above, 1)
    from_above = shifted(to_below, -1)
    received = lax.all_to_all(payload, "space", 0, 0, tiled=True)

    far_down, far_up, low_mid, high_mid = far_layers(charges, mats, own)
    far_lower, far_upper = shifted(far_up, 1), shifted(far_down, -1)

    w0, w1, coefs = kernel_modes(kernel_taps, me)
    w0 = w0.reshape(TAPS, 2, SIDE, SIDE)

    spread_out = along_z(received.reshape(COUNT * 16, SIDE), coefs)
    potentials = lax.all_to_all(spread_out.reshape(COUNT, 16, SIDE), "space", 0, 0, tiled=True)

    near_down, near_up = near_layers(charges, mats, own, from_below, from_above, spread_out)
    near_lower, near_upper = shifted(near_up, 1), shifted(near_down, -1)

    pieces = (near_down, far_down, low_mid, high_mid, far_up, near_up)
    places = ((0, 3), (3, 4), (7, 1), (8, 1), (9, 4), (13, 3))
    layers = {first + i: (k, i) for k, (first, count) in enumerate(places) for i in range(count)}
    acc = sums_along_z(pieces, layers, (0, 4, 8, 12), w0)
    acc = pltpu.with_memory_space_constraint(acc, pltpu.HBM)
    level = level_one(near_lower, near_up, near_down, near_upper, w1)
    return finish(acc, (near_lower, near_upper, far_lower, far_upper), w0, level, potentials, mats)


def solution(mesh):
    placed = (P("bead", "space", None, None), P())
    return jax.shard_map(
        body, mesh=mesh, in_specs=placed, out_specs=P("bead", "space", None, None), check_vma=False
    )
```

```python
import functools

import jax
import jax.numpy as jnp
import ml_dtypes
import numpy as np
from jax import lax
from jax.experimental import pallas as pl
from jax.experimental.pallas import tpu as pltpu
from jax.sharding import PartitionSpec as P

REACH = 7
TAPS = 15
SIDE = 128
SLAB = 16
COUNT = 32
F32 = jnp.float32
BF16 = jnp.bfloat16
CUBIC = {0: 1.0, 1: 0.5625, -1: 0.5625, 3: -0.0625, -3: -0.0625}


def symbol(side):
    theta = 2.0 * np.pi * np.arange(side) / side
    return 1.0 + 1.125 * np.cos(theta) - 0.125 * np.cos(3.0 * theta)


def split_const(matrix):
    high = matrix.astype(ml_dtypes.bfloat16)
    low = (matrix - high.astype(np.float64)).astype(ml_dtypes.bfloat16)
    return high, low


def dft_parts():
    angle = 2.0 * np.pi * (np.outer(np.arange(SIDE), np.arange(SIDE)) % SIDE) / SIDE
    c, s = np.cos(angle), np.sin(angle)
    fwd_x = np.block([[c, -s], [s, c]])
    fwd_y = np.block([[c, s], [-s, c]])
    inv_y = np.block([[c, -s], [s, c]]) / SIDE
    inv_x = np.block([[c, s], [-s, c]]) / SIDE
    return np.stack([part for m in (fwd_x, fwd_y, inv_y, inv_x) for part in split_const(m)])


def coarse_parts():
    restrict = np.zeros((64, SIDE))
    for j in range(64):
        for d, weight in CUBIC.items():
            restrict[j, (2 * j + d) % SIDE] += 0.5 * weight
    angle = 2.0 * np.pi * (np.outer(np.arange(64), np.arange(64)) % 64) / 64
    real, imag = np.cos(angle) @ restrict, -np.sin(angle) @ restrict
    along_x = np.block([[real.T, imag.T], [-imag.T, real.T]])
    along_y = np.block([[real, -imag], [imag, real]])
    xh, xl = split_const(along_x)
    yh, yl = split_const(along_y)
    return np.concatenate([np.concatenate([xh, xl], 1), yh, yl], 0)


def fold_weights():
    half = np.outer(symbol(64), symbol(64)) / 16.0
    quarter = np.outer(symbol(32), symbol(32)) / 16.0
    half = np.tile(half, (1, 2))
    quarter = np.concatenate([quarter, quarter * 0, quarter, quarter * 0], axis=1)
    return np.concatenate([half, quarter], 0).astype(np.float32)


def spread_weights():
    full = np.outer(symbol(128), symbol(128))
    half = np.tile(np.outer(symbol(64), symbol(64)), (1, 2))
    return full.astype(np.float32), half.astype(np.float32)


def split(value):
    high = value.astype(BF16)
    return high, (value - high.astype(F32)).astype(BF16)


def dot(a, b):
    return jnp.dot(a, b, preferred_element_type=F32)


def right_mul(value, high, low):
    vh, vl = split(value)
    return dot(vh, high) + dot(vl, high) + dot(vh, low)


def left_mul(high, low, value):
    vh, vl = split(value)
    return dot(high, vh) + dot(high, vl) + dot(low, vh)


def params(megabytes=16):
    return pltpu.CompilerParams(vmem_limit_bytes=megabytes * 1024 * 1024)


def whole(shape):
    return pl.BlockSpec(shape, lambda *_: (0,) * len(shape))


def forward_layer(v, mats, out):
    rows = jnp.concatenate(
        [jnp.concatenate([v[0, 0], v[1, 0]], 1), jnp.concatenate([v[2, 0], v[3, 0]], 1)], 0
    )
    a = right_mul(rows, mats[0], mats[1])
    b = jnp.concatenate(
        [
            jnp.concatenate([a[:SIDE, :SIDE], a[:SIDE, SIDE:]], 0),
            jnp.concatenate([a[SIDE:, :SIDE], a[SIDE:, SIDE:]], 0),
        ],
        1,
    )
    c = left_mul(mats[2], mats[3], b)
    out[0, 0, 0] = c[:SIDE, :SIDE]
    out[0, 0, 1] = c[SIDE:, :SIDE]
    out[0, 1, 0] = c[:SIDE, SIDE:]
    out[0, 1, 1] = c[SIDE:, SIDE:]


def near_kernel(v_low, v_high, mats, own, from_below, from_above, token, out_low, out_high):
    step = pl.program_id(0)

    @pl.when(step < 3)
    def _():
        forward_layer(v_low, mats, out_low)
        forward_layer(v_high, mats, out_high)

    cells = [own[0] + from_below[0], own[1] + from_below[1]] + [own[c] for c in range(2, 7)]
    cells += [own[7] + from_above[0], own[8] + from_above[1]]
    for half in range(2):
        @pl.when(step == 3 + half)
        def _():
            for c in range(4):
                out_high[0, c // 2, c % 2] = cells[4 * half + c]
                out_low[0, c // 2, c % 2] = cells[4 * half + c + 1]


def near_layers(charges, mats, own, from_below, from_above, token):
    shape = jax.ShapeDtypeStruct((5, 2, 2, SIDE, SIDE), F32)
    block = pl.BlockSpec((1, 2, 2, SIDE, SIDE), lambda i: (i, 0, 0, 0, 0))
    return pl.pallas_call(
        near_kernel,
        grid=(5,),
        in_specs=[
            pl.BlockSpec((4, 1, SIDE, SIDE), lambda i: (0, jnp.minimum(i, 2), 0, 0)),
            pl.BlockSpec((4, 1, SIDE, SIDE), lambda i: (0, 13 + jnp.minimum(i, 2), 0, 0)),
            pl.BlockSpec((4, 256, 256), lambda i: (0, 0, 0)),
            whole((9, SIDE, SIDE)),
            whole((2, SIDE, SIDE)),
            whole((2, SIDE, SIDE)),
            pl.BlockSpec(memory_space=pl.ANY),
        ],
        out_specs=[block, block],
        out_shape=[shape, shape],
        compiler_params=params(),
        name="near",
        cost_estimate=pl.CostEstimate(flops=1000, bytes_accessed=1000, transcendentals=0),
    )(charges, charges, mats, own, from_below, from_above, token)


def far_kernel(v_low, v_high, mats, token, out_low, out_high, mid_low, mid_high):
    step = pl.program_id(0)

    @pl.when(step < 4)
    def _():
        forward_layer(v_low, mats, out_low)
        forward_layer(v_high, mats, out_high)

    @pl.when(step == 4)
    def _():
        forward_layer(v_low, mats, mid_low)
        forward_layer(v_high, mats, mid_high)


def far_layers(charges, mats, token):
    shape = jax.ShapeDtypeStruct((4, 2, 2, SIDE, SIDE), F32)
    single = jax.ShapeDtypeStruct((1, 2, 2, SIDE, SIDE), F32)
    block = pl.BlockSpec((1, 2, 2, SIDE, SIDE), lambda i: (jnp.minimum(i, 3), 0, 0, 0, 0))
    fixed = pl.BlockSpec((1, 2, 2, SIDE, SIDE), lambda i: (0, 0, 0, 0, 0))
    return pl.pallas_call(
        far_kernel,
        grid=(5,),
        in_specs=[
            pl.BlockSpec((4, 1, SIDE, SIDE), lambda i: (0, 3 + i, 0, 0)),
            pl.BlockSpec((4, 1, SIDE, SIDE), lambda i: (0, jnp.where(i < 4, 9 + i, 8), 0, 0)),
            pl.BlockSpec((4, 256, 256), lambda i: (0, 0, 0)),
            pl.BlockSpec(memory_space=pl.ANY),
        ],
        out_specs=[block, block, fixed, fixed],
        out_shape=[shape, shape, single, single],
        compiler_params=params(),
        name="far",
        cost_estimate=pl.CostEstimate(flops=1000, bytes_accessed=1000, transcendentals=0),
    )(charges, charges, mats, token)


def fold_lanes(value, lanes):
    return value + pltpu.roll(value, SIDE - lanes, 1)


def restrict_layers(layers, first, low, high):
    out = []
    for cell in range(low, high):
        total = None
        for d, weight in CUBIC.items():
            z = 2 * cell + d - first
            if 0 <= z < len(layers):
                term = (0.5 * weight) * layers[z]
                total = term if total is None else total + term
        out.append(total)
    return out


def partial_kernel(v_hbm, mats, weights, up_ref, down_ref, own_ref, pay_ref, v_ref, mid_ref, sems):
    def copy(k):
        layers = pl.ds(2 * k, 2)
        return pltpu.make_async_copy(v_hbm.at[:, layers], v_ref.at[:, layers], sems.at[k])

    for k in range(SLAB // 2):
        copy(k).start()
    arrived = 0
    lane = lax.broadcasted_iota(jnp.int32, (SIDE, SIDE), 1)
    half, quarter = weights[:64], weights[64:]
    for c in range(-1, 10):
        while arrived < min(SLAB // 2, (2 * c + 3) // 2 + 1):
            copy(arrived).wait()
            arrived += 1
        beads = []
        for bead in range(4):
            total = None
            for d, weight in CUBIC.items():
                z = 2 * c + d
                if 0 <= z < SLAB:
                    term = (0.5 * weight) * v_ref[bead, z]
                    total = term if total is None else total + term
            beads.append(total)
        rows = jnp.concatenate([jnp.concatenate(beads[:2], 1), jnp.concatenate(beads[2:], 1)], 0)
        a = right_mul(rows, mats[:256, :SIDE], mats[:256, SIDE:])
        first, second = a[:SIDE], a[SIDE:]
        real = jnp.where(lane < 64, first, pltpu.roll(second, 64, 1))
        imag = jnp.where(lane < 64, pltpu.roll(first, 64, 1), second)
        value = left_mul(mats[256:384], mats[384:], jnp.concatenate([real, imag], 0))
        mid_ref[c + 1] = value
        if 0 <= c <= 8:
            own_ref[c] = value
        if c in (8, 9):
            up_ref[c - 8] = value
        if c in (-1, 0):
            down_ref[c + 1] = value

    small = []
    for c in range(11):
        parts = []
        for part in range(2):
            g = half * mid_ref[c, 64 * part : 64 * part + 64]
            parts.append(fold_lanes(g[:32] + g[32:], 32))
        small.append(jnp.concatenate(parts, 0))
    level2 = restrict_layers(small, -1, -2, 7)
    lane = lax.broadcasted_iota(jnp.int32, (32, SIDE), 1)
    for c, value in enumerate(level2):
        packed = jnp.where((lane // 32) % 2 == 0, value[:32], pltpu.roll(value[32:], 32, 1))
        pay_ref[:, c, :] = packed

    tiny = []
    for value in level2:
        parts = []
        for part in range(2):
            g = quarter * value[32 * part : 32 * part + 32]
            parts.append(fold_lanes(g[:16] + g[16:], 16))
        tiny.append(jnp.concatenate(parts, 0))
    level3 = restrict_layers(tiny, -2, -2, 5)
    lane = lax.broadcasted_iota(jnp.int32, (16, SIDE), 1)
    for c, value in enumerate(level3):
        packed = jnp.where((lane // 16) % 2 == 0, value[:16], pltpu.roll(value[16:], 16, 1))
        pay_ref[:, 9 + c, :] = jnp.concatenate([packed, packed], 0)


def partial_sums(charges):
    outs = [(2, SIDE, SIDE), (2, SIDE, SIDE), (9, SIDE, SIDE), (COUNT, 16, SIDE)]
    return pl.pallas_call(
        partial_kernel,
        out_shape=[jax.ShapeDtypeStruct(s, F32) for s in outs],
        in_specs=[
            pl.BlockSpec(memory_space=pltpu.HBM),
            pl.BlockSpec(memory_space=pltpu.VMEM),
            pl.BlockSpec(memory_space=pltpu.VMEM),
        ],
        scratch_shapes=[
            pltpu.VMEM((4, SLAB, SIDE, SIDE), F32),
            pltpu.VMEM((11, SIDE, SIDE), F32),
            pltpu.SemaphoreType.DMA((SLAB // 2,)),
        ],
        compiler_params=params(),
        name="partial",
        cost_estimate=pl.CostEstimate(flops=1000, bytes_accessed=1000, transcendentals=0),
    )(charges, jnp.asarray(coarse_parts()), jnp.asarray(fold_weights()))


def gather_matrix():
    def places(rows, period, shift, low, high):
        r = lax.broadcasted_iota(jnp.int32, (rows, COUNT * 16), 0)
        q = lax.broadcasted_iota(jnp.int32, (rows, COUNT * 16), 1)
        c = q % 16
        z = (period // COUNT) * (q // 16) + c - low - 2
        hit = ((r - REACH - z) % period == 0) & (c >= low) & (c < high) & (r < period + 2 * REACH)
        return jnp.where(hit, 1.0, 0.0)

    return jnp.concatenate([places(144, 128, 0, 0, 9), places(80, 64, 0, 9, 16)], 0).astype(BF16)


def scatter_matrix():
    r = lax.broadcasted_iota(jnp.int32, (COUNT * 16, 256), 0)
    q = lax.broadcasted_iota(jnp.int32, (COUNT * 16, 256), 1)
    z = 4 * (r // 16) + r % 16 - 2
    same = (z - q) % 128 == 0
    d = jnp.abs((z - 2 * (q - 128) + 64) % 128 - 64)
    weight = jnp.where(d == 0, 1.0, jnp.where(d == 1, 0.5625, jnp.where(d == 3, -0.0625, 0.0)))
    value = jnp.where(q < 128, jnp.where(same, 1.0, 0.0), jnp.where(q < 192, weight, 0.0))
    return jnp.where(r % 16 < 9, value, 0.0).astype(BF16)


def swap_lanes(value, lanes):
    lane = lax.broadcasted_iota(jnp.int32, value.shape, 1)
    return jnp.where((lane // lanes) % 2 == 0, pltpu.roll(value, SIDE - lanes, 1), pltpu.roll(value, lanes, 1))


def along_kernel(x_ref, coefs, out_ref, c_ref, s_ref):
    gather, scatter = gather_matrix(), scatter_matrix()
    a2, b2, a3, b3 = (coefs.at[pl.ds(16 * k, 16)] for k in range(4))
    spread = coefs[64:65]
    xh, xl = split(x_ref[...])
    c_ref[...] = dot(gather, xh) + dot(gather, xl)
    s_ref[:144] = swap_lanes(c_ref[:144], 32)
    s_ref[144:] = swap_lanes(c_ref[144:], 16)
    p2 = jnp.zeros((128, SIDE), F32)
    p3 = jnp.zeros((64, SIDE), F32)
    for t in range(TAPS):
        p2 = p2 + a2[t : t + 1] * c_ref[t : t + 128] + b2[t : t + 1] * s_ref[t : t + 128]
        p3 = p3 + a3[t : t + 1] * c_ref[144 + t : 208 + t] + b3[t : t + 1] * s_ref[144 + t : 208 + t]
    block = (lax.broadcasted_iota(jnp.int32, p3.shape, 1) // 16) % 4
    wide = jnp.where(block == 0, p3, jnp.where(block == 3, pltpu.roll(p3, 32, 1), pltpu.roll(p3, 16, 1)))
    wide = spread * wide
    both = jnp.concatenate([p2, wide, jnp.zeros((64, SIDE), F32)], 0)
    bh, bl = split(both)
    out_ref[...] = dot(scatter, bh) + dot(scatter, bl)


def along_z(received, coefs):
    return pl.pallas_call(
        along_kernel,
        out_shape=jax.ShapeDtypeStruct((COUNT * 16, SIDE), F32),
        scratch_shapes=[pltpu.VMEM((224, SIDE), F32), pltpu.VMEM((224, SIDE), F32)],
        compiler_params=params(),
        name="along",
        cost_estimate=pl.CostEstimate(flops=100000000000, bytes_accessed=400000000, transcendentals=0),
    )(received, coefs)


def level_kernel(below, own, last, above, w_ref, p_ref):
    def cell_ref(c):
        ref, c = (below, c + 8) if c < 0 else (own, c) if c < 8 else (last, 7) if c == 8 else (above, c - 9)
        return ref, (3 + c // 4, c // 2 % 2, c % 2)

    def block(r, carry):
        rows = pl.ds(pl.multiple_of(8 * r, 8), 8)
        lower = pl.ds(pl.multiple_of(64 + 8 * r, 8), 8)
        for first, outputs in ((-1, 6), (5, 5)):
            def value(j):
                ref, i = cell_ref(first + j - REACH)
                return ref[(*i, rows)], ref[(*i, lower)]

            sums = slide(outputs, 1, value, lambda t: (w_ref[t, rows], w_ref[t, lower]))
            for i in range(outputs):
                p_ref[first + i + 1, rows] = sums[i][0]
                p_ref[first + i + 1, lower] = sums[i][1]
        return carry

    lax.fori_loop(0, 8, block, 0)


def level_one(below, own, last, above, w1):
    return pl.pallas_call(
        level_kernel,
        out_shape=jax.ShapeDtypeStruct((11, SIDE, SIDE), F32),
        compiler_params=params(),
        name="level",
        cost_estimate=pl.CostEstimate(flops=1000, bytes_accessed=1000, transcendentals=0),
    )(below, own, last, above, w1)


def spread_levels(level, y_ref, spread, out_ref, p_ref):
    lane = lax.broadcasted_iota(jnp.int32, (32, SIDE), 1)
    low = (lane // 32) % 2 == 0
    wides = []
    for c in range(9):
        y = y_ref[:, c, :]
        re = jnp.where(low, y, pltpu.roll(y, 32, 1))
        im = jnp.where(low, pltpu.roll(y, SIDE - 32, 1), y)
        wides.append((re, im))
    for c in range(-1, 10):
        for part in range(2):
            total = None
            for d, weight in CUBIC.items():
                if (c - d) % 2 == 0 and -2 <= (c - d) // 2 <= 6:
                    term = weight * wides[(c - d) // 2 + 2][part]
                    total = term if total is None else total + term
            for tile in range(2):
                rows = slice(64 * part + 32 * tile, 64 * part + 32 * tile + 32)
                p_ref[c + 1, rows] = level[c + 1, rows] + spread[32 * tile : 32 * tile + 32] * total
    for z in range(SLAB):
        total = None
        for d, weight in CUBIC.items():
            if (z - d) % 2 == 0:
                term = weight * p_ref[(z - d) // 2 + 1]
                total = term if total is None else total + term
        out_ref[z] = total


def sums_kernel(layers, groups, added, *refs):
    start = refs[0]
    refs = refs[1:] if added else refs
    sources, w_ref, out = refs[:-2], refs[-2], refs[-1]
    for k, z in enumerate(groups):
        def block(r, carry):
            rows = pl.ds(pl.multiple_of(8 * r, 8), 8)

            def value(j):
                if z + j - REACH not in layers:
                    return None
                n, i = layers[z + j - REACH]
                return [sources[n][i, pair, part, rows] for pair in range(2) for part in range(2)]

            sums = slide(4, 2, value, lambda t: (w_ref[t, 0, rows], w_ref[t, 1, rows]))
            for i in range(4):
                for n in range(4):
                    total = sums[i][n]
                    if added:
                        before = start[4 * k + i, n // 2, n % 2, rows]
                        total = before if total is None else before + total
                    out[4 * k + i, n // 2, n % 2, rows] = total
            return carry

        lax.fori_loop(0, SIDE // 8, block, 0)


def sums_along_z(pieces, layers, groups, w0, start=None):
    return pl.pallas_call(
        functools.partial(sums_kernel, layers, groups, start is not None),
        out_shape=jax.ShapeDtypeStruct((4 * len(groups), 2, 2, SIDE, SIDE), F32),
        compiler_params=params(24),
        name="sums",
        cost_estimate=pl.CostEstimate(flops=1000, bytes_accessed=1000, transcendentals=0),
    )(*(() if start is None else (start,)), *pieces, w0)


def finish_kernel(
    acc, far_low, far_high, w_ref, level, y_ref, small, spread, mats, out, coarse, p_ref, sum_ref
):
    step = pl.program_id(0)

    @pl.when(step == 0)
    def _():
        spread_levels(level, y_ref, small, coarse, p_ref)

    halo = [(far_low, k, k - 7) for k in range(4)] + [(far_high, k, 19 + k) for k in range(4)]

    def add_halo(first):
        def block(r, carry):
            rows = pl.ds(pl.multiple_of(8 * r, 8), 8)
            for i in range(2):
                sums = [acc[i, pair, part, rows] for pair in range(2) for part in range(2)]
                for ref, k, z in halo:
                    t = z - first - i + REACH
                    if not 0 <= t < TAPS:
                        continue
                    wr, wi = w_ref[t, 0, rows], w_ref[t, 1, rows]
                    for pair in range(2):
                        vr, vi = ref[k, pair, 0, rows], ref[k, pair, 1, rows]
                        sums[2 * pair] += wr * vr - wi * vi
                        sums[2 * pair + 1] += wr * vi + wi * vr
                for n in range(4):
                    sum_ref[i, n // 2, n % 2, rows] = sums[n]
            return carry

        lax.fori_loop(0, SIDE // 8, block, 0)

    for number, first in ((4, 0), (5, 2), (6, 12), (7, 14)):
        @pl.when(step == number)
        def _():
            add_halo(first)

    lane = lax.broadcasted_iota(jnp.int32, (64, SIDE), 1)
    z = 2 * pair_of_layers(step)

    def run(modes):
        columns = []
        for i in range(2):
            sides = [[], []]
            for part in range(2):
                g = coarse[z + i, 64 * part : 64 * part + 64]
                h = pltpu.roll(g, 64, 1)
                for pair in range(2):
                    tile = jnp.where((lane < 64) == (pair == 0), g, h)
                    for row in (0, 64):
                        sides[pair].append(modes[i, pair, part, row : row + 64] + spread[row : row + 64] * tile)
            columns += [jnp.concatenate(side, 0) for side in sides]
        c = left_mul(mats[0], mats[1], jnp.concatenate(columns, 1))
        rows = jnp.concatenate(
            [
                jnp.concatenate([c[:SIDE, SIDE * n : SIDE * n + SIDE], c[SIDE:, SIDE * n : SIDE * n + SIDE]], 1)
                for n in range(4)
            ],
            0,
        )
        d = right_mul(rows, mats[2], mats[3])
        for n in range(4):
            for half in range(2):
                out[2 * (n % 2) + half, n // 2] = d[SIDE * n : SIDE * n + SIDE, SIDE * half : SIDE * half + SIDE]

    @pl.when(step < 4)
    def _():
        run(acc)

    @pl.when(step >= 4)
    def _():
        run(sum_ref)


def pair_of_layers(step):
    return jnp.where(step < 4, 2 + step, jnp.where(step < 6, step - 4, step))


def finish(acc, halos, w0, level, potentials, mats):
    full, half = spread_weights()
    tables = [pltpu.with_memory_space_constraint(jnp.asarray(t), pltpu.HBM) for t in (half, full)]
    return pl.pallas_call(
        finish_kernel,
        grid=(8,),
        in_specs=[
            pl.BlockSpec((2, 2, 2, SIDE, SIDE), lambda i: (pair_of_layers(i), 0, 0, 0, 0)),
            whole((4, 2, 2, SIDE, SIDE)),
            whole((4, 2, 2, SIDE, SIDE)),
            whole((TAPS, 2, SIDE, SIDE)),
            whole((11, SIDE, SIDE)),
            whole((COUNT, 16, SIDE)),
            whole((64, SIDE)),
            whole((SIDE, SIDE)),
            pl.BlockSpec((4, 256, 256), lambda i: (1, 0, 0)),
        ],
        out_specs=pl.BlockSpec((4, 2, SIDE, SIDE), lambda i: (0, pair_of_layers(i), 0, 0)),
        out_shape=jax.ShapeDtypeStruct((4, SLAB, SIDE, SIDE), F32),
        scratch_shapes=[
            pltpu.VMEM((SLAB, SIDE, SIDE), F32),
            pltpu.VMEM((11, SIDE, SIDE), F32),
            pltpu.VMEM((2, 2, 2, SIDE, SIDE), F32),
        ],
        compiler_params=params(28),
        name="finish",
        cost_estimate=pl.CostEstimate(flops=1000, bytes_accessed=1000, transcendentals=0),
    )(acc, *halos, w0, level, potentials, *tables, mats)


def slide(outputs, pairs, value, weight):
    sums = [[None] * (2 * pairs) for _ in range(outputs)]
    window = {}
    for j in range(outputs + TAPS - 1):
        if j < TAPS:
            window[j] = weight(j)
        v = value(j)
        for i in range(outputs if v is not None else 0):
            t = j - i
            if not 0 <= t < TAPS:
                continue
            wr, wi = window[t]
            for pair in range(pairs):
                vr, vi = v[2 * pair], v[2 * pair + 1]
                for k, term in ((2 * pair, wr * vr - wi * vi), (2 * pair + 1, wr * vi + wi * vr)):
                    sums[i][k] = term if sums[i][k] is None else sums[i][k] + term
    return sums


def shifted(value, steps):
    pairs = [(source, (source + steps) % COUNT) for source in range(COUNT)]
    return lax.ppermute(value, "space", pairs)


def wave_table():
    columns = []
    for side in (128, 64, 32, 16):
        offset = np.arange(SIDE) % max(side, 64)
        lanes = np.where(offset < 2 * side, offset % side, -1)
        angle = 2.0 * np.pi * np.outer(np.arange(TAPS) - REACH, lanes) / side
        columns += [np.where(lanes >= 0, np.cos(angle), 0.0), np.where(lanes >= 0, np.sin(angle), 0.0)]
    return np.concatenate(columns, 1).astype(np.float32)


def modes_kernel(me_ref, taps_ref, rows_ref, cols_ref, z_ref, w0_ref, w1_ref, coef_ref):
    def row(level, term, dim, part):
        return rows_ref[pl.ds((level * 4 + term) * 3 + dim, 1), pl.ds((2 * level + part) * SIDE, SIDE)]

    for level, w_ref, side in ((0, w0_ref, 128), (1, w1_ref, 64)):
        for block in range(0, side, 32):
            real, imag = [], []
            for term in range(4):
                column = (level * 4 + term) * 3 + 1
                yr = cols_ref[pl.ds(2 * level * SIDE + block, 32), pl.ds(column, 1)]
                yi = cols_ref[pl.ds((2 * level + 1) * SIDE + block, 32), pl.ds(column, 1)]
                xr, xi = row(level, term, 2, 0), row(level, term, 2, 1)
                real.append(yr * xr - yi * xi)
                imag.append(yr * xi + yi * xr)

            def tap(t, carry):
                for part, values in ((0, real), (1, imag)):
                    total = None
                    for term in range(4):
                        scaled = taps_ref[(level * 4 + term) * TAPS + t] * values[term]
                        total = scaled if total is None else total + scaled
                    w_ref[t, pl.ds(part * side + block, 32)] = total
                return carry

            lax.fori_loop(0, TAPS, tap, 0)

    me = me_ref[0]
    coef_ref[...] = jnp.zeros_like(coef_ref)
    for level, base, side in ((2, 0, 32), (3, 32, 16)):
        lane = lax.broadcasted_iota(jnp.int32, (1, SIDE), 1)
        sign = jnp.where((lane // side) % 2 == 0, -1.0, 1.0)
        chosen = lane == lax.rem(me, side)
        a = b = None
        for term in range(4):
            yr = jnp.sum(jnp.where(chosen, row(level, term, 1, 0), 0.0), axis=1, keepdims=True)
            yi = jnp.sum(jnp.where(chosen, row(level, term, 1, 1), 0.0), axis=1, keepdims=True)
            xr, xi = row(level, term, 2, 0), row(level, term, 2, 1)
            z = z_ref[:, pl.ds(level * 4 + term, 1)]
            ta = z * (yr * xr - yi * xi)
            tb = z * (sign * (yr * xi + yi * xr))
            a = ta if a is None else a + ta
            b = tb if b is None else b + tb
        coef_ref[pl.ds(base, TAPS)] = a
        coef_ref[pl.ds(base + 16, TAPS)] = b
    lane = lax.broadcasted_iota(jnp.int32, (1, SIDE), 1)
    theta = (lane % 32).astype(F32) * (2.0 * np.pi / 32)
    symbols = 1.0 + 1.125 * jnp.cos(theta) - 0.125 * jnp.cos(3.0 * theta)
    chosen = jnp.sum(jnp.where(lane == me, symbols, 0.0), axis=1, keepdims=True)
    coef_ref[pl.ds(64, 1)] = symbols * chosen


def kernel_modes(taps, me):
    table = jnp.asarray(wave_table())
    flat = taps.reshape(48, TAPS)
    z = taps[:, :, 0].reshape(16, TAPS)
    exact = lax.Precision.HIGHEST
    rows = jnp.dot(flat, table, precision=exact)
    cols = jnp.dot(jnp.asarray(wave_table().T), flat.T, precision=exact)
    outs = [(TAPS, 256, SIDE), (TAPS, SIDE, SIDE), (80, SIDE)]
    in_smem = pl.BlockSpec(memory_space=pltpu.SMEM)
    in_vmem = pl.BlockSpec(memory_space=pltpu.VMEM)
    return pl.pallas_call(
        modes_kernel,
        in_specs=[in_smem, in_smem, in_vmem, in_vmem, in_vmem],
        out_shape=[jax.ShapeDtypeStruct(s, F32) for s in outs],
        compiler_params=params(),
        name="modes",
        cost_estimate=pl.CostEstimate(flops=1000, bytes_accessed=1000, transcendentals=0),
    )(me.reshape(1), z.reshape(-1), rows, cols, z.T)


def body(charges, kernel_taps):
    mats = jnp.asarray(dft_parts())
    charges = pltpu.with_memory_space_constraint(charges, pltpu.HBM)
    me = lax.axis_index("space")

    to_above, to_below, own, payload = partial_sums(charges)
    from_below = shifted(to_above, 1)
    from_above = shifted(to_below, -1)
    received = lax.all_to_all(payload, "space", 0, 0, tiled=True)

    far_down, far_up, low_mid, high_mid = far_layers(charges, mats, own)
    far_lower, far_upper = shifted(far_up, 1), shifted(far_down, -1)

    w0, w1, coefs = kernel_modes(kernel_taps, me)
    w0 = w0.reshape(TAPS, 2, SIDE, SIDE)

    spread_out = along_z(received.reshape(COUNT * 16, SIDE), coefs)
    potentials = lax.all_to_all(spread_out.reshape(COUNT, 16, SIDE), "space", 0, 0, tiled=True)

    near_down, near_up = near_layers(charges, mats, own, from_below, from_above, spread_out)
    near_lower, near_upper = shifted(near_up, 1), shifted(near_down, -1)

    pieces = (near_down, far_down, low_mid, high_mid, far_up, near_up)
    places = ((0, 3), (3, 4), (7, 1), (8, 1), (9, 4), (13, 3))
    layers = {first + i: (k, i) for k, (first, count) in enumerate(places) for i in range(count)}
    acc = sums_along_z(pieces, layers, (0, 4, 8, 12), w0)
    halo = {z: (k, i) for k, first in enumerate((-3, 16)) for i, z in enumerate(range(first, first + 3))}
    acc = sums_along_z((near_lower, near_upper), halo, (0, 4, 8, 12), w0, acc)
    acc = pltpu.with_memory_space_constraint(acc, pltpu.HBM)
    level = level_one(near_lower, near_up, near_down, near_upper, w1)
    level = pltpu.with_memory_space_constraint(level, pltpu.HBM)
    return finish(acc, (far_lower, far_upper), w0, level, potentials, mats)


def solution(mesh):
    placed = (P("bead", "space", None, None), P())
    return jax.shard_map(
        body, mesh=mesh, in_specs=placed, out_specs=P("bead", "space", None, None), check_vma=False
    )
```
